256 devices in a mesh: ctx: 32 (over z, x_lo, core), head: 8 (over x_hi, y).
Axes of the slice: x: 4 (x_hi: 2, x_lo: 2; x = x_hi * 2 + x_lo), y: 4, z: 8, core: 2. Of those that a mesh axis runs over, the one named last changes fastest.
Arguments:
- kv_latent: bfloat16 [16384, 576], P('ctx'), may hold values from -4 to 4
- queries: bfloat16 [16384, 3072], P('ctx', 'head'), may hold values from -22 to 22
- grad_out: bfloat16 [16384, 2048], P('ctx', 'head'), may hold values from -6 to 6
- kv_up_weight: bfloat16 [512, 4096], P(None, 'head'), may hold values from -0.25 to 0.25
- doc_ids: int32 [16384], replicated, may hold values from 0 to 15, never falling along the last dimension, each value on 1 to 1536 neighbouring positions
Outputs:
- grad_queries: bfloat16 [16384, 3072], P('ctx', 'head')
- grad_latent: bfloat16 [16384, 576], P('ctx')
- grad_weight: float32 [512, 4096], P('ctx', 'head')
The draws below stay inside these ranges and needn't reach their ends.
Inputs may be any that keep to these rules, and one draw needn't show every extreme that they name: `doc_ids`: document ids never fall along the sequence; every document has 1 to 1536 tokens, and one has exactly 1536.
All inputs are finite; a program needn't handle non-finite values.
Results may differ from the reference program's by a relative error of at most 0.0076.
Values may be sent and summed in bfloat16 or wider, within the bound.
A program may use at most 64 MiB of HBM per device.

```python
import math
import jax
import jax.numpy as jnp
import numpy as np
from jax import lax

HEADS = 16
NOPE = 128
ROPE = 64
VDIM = 128
LATENT = 512
TOK_DEV = 512
REACH = 3
TOKENS = 16384
DOCS = 16
DOC_MOST = 1536


def draw_kv_latent(key, part):
    inner_key = jax.random.fold_in(key, 1)
    values = jnp.clip(jax.random.normal(inner_key, (TOKENS, LATENT + ROPE), jnp.float32), -4.0, 4.0)
    return values.astype(jnp.bfloat16)


def draw_queries(key, part):
    inner_key = jax.random.fold_in(key, 2)
    values = jnp.clip(jax.random.normal(inner_key, (TOKENS, HEADS * (NOPE + ROPE)), jnp.float32), -4.0, 4.0)
    return values.astype(jnp.bfloat16)


def block_scale(own_key, extent, cuts, smallest, top_value):
    def one(axis_at, blocks):
        heights = jax.random.uniform(jax.random.fold_in(jax.random.fold_in(own_key, 6), axis_at), (blocks,), jnp.float32, smallest / len(cuts), top_value / len(cuts))
        return jnp.repeat(jnp.exp(heights), extent[axis_at] // blocks).reshape((-1,) + (1,) * (len(extent) - axis_at - 1))

    gain = one(*cuts[0])
    for cut in cuts[1:]:
        gain = gain * one(*cut)
    return gain


def length_profile(count, total, most, skew):
    portions = [(1 << 20) // math.isqrt(grade ** skew) + 1 for grade in range(2, count + 1)]
    surplus, counts = total - most - (count - 1), [1] * (count - 1)
    while surplus > 0:
        movable = [i for i in range(count - 1) if counts[i] < most]
        mass, left = sum([portions[i] for i in movable]), surplus
        for i in movable:
            more = min(most - counts[i], max(1, left * portions[i] // mass), surplus)
            counts[i] = counts[i] + more
            surplus = surplus - more
    return np.array([most] + counts)


def ragged(own_key, amount, total, reach, slope):
    if amount == 2:
        one = jax.random.randint(own_key, (), max(1, total - reach), min(reach, total - 1) + 1)
        return jnp.stack([one, total - one])
    lengths = jnp.asarray(length_profile(amount, total, reach, slope), jnp.int32)
    twos = (amount - 1) // 2
    source_of, receiver = lengths[1:1 + 2 * twos:2], lengths[2:2 + 2 * twos:2]
    margin = jnp.minimum(source_of - 1, reach - receiver)
    shifted = jax.random.randint(jax.random.fold_in(own_key, 1), (twos,), 0, 1 << 20) % (margin + 1)
    lengths = lengths.at[1:1 + 2 * twos:2].set(source_of - shifted).at[2:2 + 2 * twos:2].set(receiver + shifted)
    return lengths[jax.random.permutation(jax.random.fold_in(own_key, 2), amount)]


def normal_values(stream_key, dims, spread, reach, pieces=(), held_as=jnp.bfloat16):
    drawn = spread * jax.random.normal(stream_key, dims, jnp.float32)
    if pieces:
        drawn = drawn * block_scale(stream_key, dims, pieces, -0.22, 0.18)
    return jnp.clip(drawn, -reach, reach).astype(held_as)


def setup_inputs(seed: int = 0) -> dict:
    streams_of = jax.random.split(jax.random.key(seed), 6)
    kv_latent = draw_kv_latent(jax.random.fold_in(streams_of[5], 71), 0)
    queries = draw_queries(jax.random.fold_in(streams_of[5], 71), 0)
    grad_out = normal_values(streams_of[2], (TOKENS, HEADS * VDIM), 1.0, 6.0, ((0, 32), (1, 8)))
    kv_up_weight = normal_values(streams_of[3], (LATENT, HEADS * (NOPE + VDIM)), LATENT ** -0.5, 0.25, ((1, 8),))
    doc_ids = jnp.searchsorted(jnp.cumsum(ragged(streams_of[4], DOCS, TOKENS, DOC_MOST, 1)), jnp.arange(TOKENS), side="right").astype(jnp.int32)
    return {"kv_latent": kv_latent, "queries": queries, "grad_out": grad_out, "kv_up_weight": kv_up_weight, "doc_ids": doc_ids}


masked_score = -1e+30

def reference(kv_latent, queries, grad_out, kv_up_weight, doc_ids):
    score_scale = 1.0 / math.sqrt(NOPE + ROPE)
    span = (REACH + 1) * TOK_DEV
    latent = kv_latent[:, :LATENT]
    rope_keys = kv_latent[:, LATENT:].astype(jnp.float32)
    lifted = jnp.dot(latent, kv_up_weight, preferred_element_type=jnp.float32).astype(jnp.bfloat16)
    lifted = lifted.reshape(TOKENS, HEADS, NOPE + VDIM).astype(jnp.float32)
    head_queries = queries.reshape(TOKENS, HEADS, NOPE + ROPE).astype(jnp.float32)
    head_grads = grad_out.reshape(TOKENS, HEADS, VDIM).astype(jnp.float32)

    def one_block(carry, block_index):
        key_total, rope_total = carry
        query_start = (block_index * TOK_DEV).astype(jnp.int32)
        key_start = jnp.maximum(query_start - REACH * TOK_DEV, 0).astype(jnp.int32)
        query_rows = lax.dynamic_slice_in_dim(head_queries, query_start, TOK_DEV, 0)
        out_rows = lax.dynamic_slice_in_dim(head_grads, query_start, TOK_DEV, 0)
        key_rows = lax.dynamic_slice_in_dim(lifted, key_start, span, 0)
        rope_rows = lax.dynamic_slice_in_dim(rope_keys, key_start, span, 0)
        query_pos = query_start + jnp.arange(TOK_DEV, dtype=jnp.int32)
        key_pos = key_start + jnp.arange(span, dtype=jnp.int32)
        query_docs = lax.dynamic_slice_in_dim(doc_ids, query_start, TOK_DEV)
        key_docs = lax.dynamic_slice_in_dim(doc_ids, key_start, span)
        visible = (query_docs[:, None] == key_docs[None, :]) & (key_pos[None, :] <= query_pos[:, None])
        key_nope = key_rows[:, :, :NOPE]
        values = key_rows[:, :, NOPE:]
        query_nope = query_rows[:, :, :NOPE]
        query_rope = query_rows[:, :, NOPE:]
        scores = score_scale * (jnp.einsum('thd,khd->htk', query_nope, key_nope) + jnp.einsum('thd,kd->htk', query_rope, rope_rows))
        scores = jnp.where(visible[None], scores, masked_score)
        row_top = lax.optimization_barrier(jnp.max(scores, axis=2))
        log_total = row_top + jnp.log(lax.optimization_barrier(jnp.sum(jnp.exp(scores - row_top[:, :, None]), axis=2)))
        weights = jnp.where(visible[None], jnp.exp(scores - log_total[:, :, None]), 0.0)
        grad_probs = jnp.einsum('thd,khd->htk', out_rows, values)
        delta = lax.optimization_barrier(jnp.sum(weights * grad_probs, axis=2))
        grad_scores = lax.optimization_barrier((weights * (grad_probs - delta[:, :, None])).astype(jnp.bfloat16)).astype(jnp.float32)
        weights_low = lax.optimization_barrier(weights.astype(jnp.bfloat16)).astype(jnp.float32)
        grad_query = score_scale * jnp.concatenate([jnp.einsum('htk,khd->thd', grad_scores, key_nope), jnp.einsum('htk,kd->thd', grad_scores, rope_rows)], axis=2)
        grad_keys = score_scale * jnp.einsum('htk,thd->khd', grad_scores, query_nope)
        grad_values = jnp.einsum('htk,thd->khd', weights_low, out_rows)
        grad_rope = score_scale * jnp.einsum('htk,thd->kd', grad_scores, query_rope)
        block_kv = jnp.concatenate([grad_keys, grad_values], axis=2)
        key_total = lax.dynamic_update_slice_in_dim(key_total, lax.dynamic_slice_in_dim(key_total, key_start, span, 0) + block_kv, key_start, 0)
        rope_total = lax.dynamic_update_slice_in_dim(rope_total, lax.dynamic_slice_in_dim(rope_total, key_start, span, 0) + grad_rope, key_start, 0)
        return ((key_total, rope_total), grad_query)
    start_sums = (jnp.zeros((TOKENS, HEADS, NOPE + VDIM), jnp.float32), jnp.zeros((TOKENS, ROPE), jnp.float32))
    (key_total, rope_total), query_grads = lax.scan(one_block, start_sums, jnp.arange(TOKENS // TOK_DEV, dtype=jnp.int32))
    grad_queries = query_grads.reshape(TOKENS, HEADS * (NOPE + ROPE)).astype(jnp.bfloat16)
    kv_grad = key_total.reshape(TOKENS, HEADS * (NOPE + VDIM)).astype(jnp.bfloat16)
    latent_grad = jnp.dot(kv_grad, kv_up_weight.T, preferred_element_type=jnp.float32)
    grad_latent = jnp.concatenate([latent_grad, rope_total], axis=1).astype(jnp.bfloat16)
    grad_weight = jnp.dot(latent.T, kv_grad, preferred_element_type=jnp.float32)
    return (grad_queries, grad_latent, grad_weight)
```

```python
import math

import jax
import jax.numpy as jnp
from jax import lax
from jax.experimental import pallas as pl
from jax.experimental.pallas import tpu as pltpu
from jax.sharding import PartitionSpec as P

NOPE, ROPE, VDIM, LATENT = 128, 64, 128, 512
ROWS = 512
HEADS = 2
BIG = 1e30
MESH = pl.DeviceIdType.MESH
SCALE = 1.0 / math.sqrt(NOPE + ROPE)
WIDE = LATENT + ROPE
F32, BF16 = jnp.float32, jnp.bfloat16


def mm(a, b):
    return jnp.dot(a, b, preferred_element_type=F32)


def body(
    latx, q, do, w, dq_ref, out_ref, gwo_ref,
    kbuf, relay_buf, qcat, qcat_t, do_t, w_t, lat_t, kc_t, e_buf, g_buf, m_ref, l_ref, x_ref, mref,
    dq_t, gw, sbuf, crecv, ysum, yrecv, tbuf, orecv, fin, g1recv, g2buf, g2recv, g3buf, g3recv,
    s_p1, s_rel, s_core, s_y, s_o, s_ag, s_g, r_slot, r_rel, r_core, r_y, r_o, r_ag, r_g,
):
    ctx = lax.axis_index("ctx")
    head = lax.axis_index("head")
    z, xl, co = ctx // 4, (ctx // 2) % 2, ctx % 2
    xh, y = head // 4, head % 4
    chip = ctx // 2

    def dev(z_, xl_, co_, xh_, y_):
        return (z_ * 4 + xl_ * 2 + co_, xh_ * 4 + y_)

    def copy(src, dst, ss, rs, to):
        return pltpu.make_async_remote_copy(
            src_ref=src, dst_ref=dst, send_sem=ss, recv_sem=rs, device_id=to, device_id_type=MESH
        )

    barrier = pltpu.get_barrier_semaphore()
    partners = [(ctx, (head + t) % 8) for t in range(1, 8)]
    partners += [dev(z, 1 - xl, co, u // 4, u % 4) for u in range(8)]
    partners += [dev((z + t) % 8, xl, co, xh, y) for t in range(1, 8)]
    partners += [dev(z, xl, 1 - co, u, y) for u in range(2)]
    partners += [dev(z, 1 - xl, 1 - co, u, y) for u in range(2)]
    for dz in (1, 7):
        partners += [dev((z + dz) % 8, 1 - xl, k, u, y) for k in range(2) for u in range(2)]
        partners += [dev((z + dz) % 8, xl, 1 - co, u, y) for u in range(2)]
        partners += [dev((z + dz) % 8, xl, co, 1 - xh, y)]
    for to in partners:
        pl.semaphore_signal(barrier, inc=1, device_id=to, device_id_type=MESH)

    kbuf[3] = latx[...]
    query_mask = ((latx[:, WIDE:].astype(F32) - 1.0) * BIG).astype(BF16)
    for h in range(HEADS):
        base = h * (NOPE + ROPE)
        qc = jnp.concatenate([q[:, base : base + NOPE + ROPE], query_mask], axis=1)
        qcat[h] = qc
        qcat_t[h] = qc.T
        do_t[h] = do[:, h * VDIM : (h + 1) * VDIM].T
    w_t[...] = w[...].T

    pl.semaphore_wait(barrier, len(partners))

    sibling = dev(z, xl, 1 - co, xh, y)
    first = jnp.where(co == 1, 2, 0)
    direct = jnp.where(xl == 0, jnp.where(co == 0, 2, 0), 1)
    third = 3 - first - direct

    def full():
        slot = jnp.where(co == 0, 2, 0)
        return copy(latx, kbuf.at[slot], s_p1.at[0], r_slot.at[slot], dev((z + co) % 8, xl, 1 - co, xh, y))

    def piece():
        rows = pl.ds(pl.multiple_of(head * 64, 64), 64)
        return copy(latx.at[rows], relay_buf, s_p1.at[1], r_rel.at[0], dev((z + 1) % 8, 1, 1 - co, xh, y))

    def half(d):
        rows = pl.ds(d * 256, 256)
        return copy(latx.at[rows], kbuf.at[1, rows], s_p1.at[2 + d], r_slot.at[1], dev(z, 1, co, (xh + d) % 2, y))

    def relay(t):
        slot = jnp.where(co == 0, 2, 0)
        rows = pl.ds(pl.multiple_of(head * 64, 64), 64)
        return copy(relay_buf, kbuf.at[slot, rows], s_rel.at[t], r_slot.at[slot], (z * 4 + co, (head + t) % 8))

    def forward():
        slot = jnp.where(xl == 0, 1, jnp.where(co == 0, 0, 2))
        return copy(kbuf.at[direct], kbuf.at[slot], s_p1.at[4], r_slot.at[slot], sibling)

    @pl.when(xl == 1)
    def _():
        piece().start()

    full().start()

    @pl.when(xl == 0)
    def _():
        half(0).start()
        half(1).start()

    def wait_slot(s):
        copy(latx, kbuf.at[s], s_p1.at[0], r_slot.at[s], sibling).wait_recv()

    def stream(s, own):
        lat = kbuf[s, :, :LATENT]
        tail = kbuf[s, :, LATENT:]
        kv = mm(lat, w[...]).astype(BF16)
        lat_t[s] = lat.T
        for h in range(HEADS):
            base = h * (NOPE + VDIM)
            kc = jnp.concatenate([kv[:, base : base + NOPE], tail], axis=1)
            kc_t[s, h] = kc.T
            scores = mm(kc, qcat_t[h]) * (SCALE * math.log2(math.e))
            if own:
                key = lax.broadcasted_iota(jnp.int32, (ROWS, ROWS), 0)
                query = lax.broadcasted_iota(jnp.int32, (ROWS, ROWS), 1)
                scores = jnp.where(key <= query, scores, -BIG)
            top = jnp.max(scores, axis=0, keepdims=True)
            if not own:
                top = jnp.maximum(top, m_ref[h])
            e = jnp.exp2(scores - top)
            g = mm(kv[:, base + NOPE : base + NOPE + VDIM], do_t[h])
            mass = jnp.sum(e, axis=0, keepdims=True)
            cross = jnp.sum(e * g, axis=0, keepdims=True)
            if not own:
                factor = jnp.exp2(m_ref[h] - top)
                mass = mass + l_ref[h] * factor
                cross = cross + x_ref[h] * factor
            m_ref[h] = top
            l_ref[h] = mass
            x_ref[h] = cross
            mref[s, h] = top
            e_buf[s, h] = e
            g_buf[s, h] = g

    @pl.when(xl == 1)
    def _():
        piece().wait_recv()
        for t in range(8):
            relay(t).start()

    stream(3, True)
    wait_slot(first)
    stream(first, False)
    wait_slot(direct)
    forward().start()
    stream(direct, False)
    wait_slot(third)
    stream(third, False)

    zero = jnp.zeros((256, WIDE), BF16)

    @pl.when(co == 0)
    def _():
        crecv[0] = zero
        sbuf[4, 0] = zero
        orecv[:, 2] = jnp.zeros((2, 2, 32, WIDE), BF16)

    @pl.when(co == 1)
    def _():
        crecv[4] = zero
        sbuf[0, 1] = zero

    def second(s):
        grad_rope = None
        parts = []
        for h in range(HEADS):
            inverse = 1.0 / l_ref[h]
            delta = x_ref[h] * inverse
            p = e_buf[s, h] * (jnp.exp2(mref[s, h] - m_ref[h]) * inverse)
            ds = (p * (g_buf[s, h] - delta)).astype(BF16)
            pb = p.astype(BF16)
            grad_q = mm(kc_t[s, h], ds)
            if s == 0:
                dq_t[h] = grad_q
            else:
                dq_t[h] += grad_q
            grad_k = mm(ds, qcat[h]) * SCALE
            grad_v = mm(pb, do[:, h * VDIM : (h + 1) * VDIM])
            parts += [grad_k[:, :NOPE], grad_v]
            rope = grad_k[:, NOPE : NOPE + ROPE]
            grad_rope = rope if grad_rope is None else grad_rope + rope
        dkv = jnp.concatenate(parts, axis=1).astype(BF16)
        grad = jnp.concatenate([mm(dkv, w_t[...]), grad_rope], axis=1)
        sbuf[s + co] = grad.astype(BF16).reshape(2, 256, WIDE)
        part = mm(lat_t[s], dkv).reshape(16, 2, 16, 512)
        if s == 0:
            gw[...] = part
        else:
            gw[...] += part

    def core_send(s):
        a = s + co
        return copy(sbuf.at[a, 1 - co], crecv.at[a], s_core.at[s], r_core.at[a], sibling)

    def y_send(a, t):
        to = (y + t) % 4
        return copy(ysum.at[a, to], yrecv.at[a, t - 1], s_y.at[a, t - 1], r_y.at[a, t - 1], dev(z, xl, co, xh, to))

    def finish(a):
        def wait():
            copy(sbuf.at[a, 0], crecv.at[a], s_core.at[0], r_core.at[a], sibling).wait_recv()

        if a == 0:
            pl.when(co == 1)(wait)
        elif a == 4:
            pl.when(co == 0)(wait)
        else:
            wait()
        total = sbuf[a, co].astype(F32) + crecv[a].astype(F32)
        ysum[a] = total.astype(BF16).reshape(4, 64, WIDE)
        for t in (2, 1, 3):
            y_send(a, t).start()

    def o_send(a, d):
        owner = (2 * chip + 29 + a) % 32
        to = (xh + d) % 2
        return copy(
            tbuf.at[a, to], orecv.at[xh, a // 2, co], s_o.at[a, d], r_o.at[xh, a // 2, co], (owner, to * 4 + y)
        )

    def o_each(a, d, remote, here):
        if d == 0 and a >= 3:
            pl.when(co != a - 3)(remote)
            if here is not None:
                pl.when(co == a - 3)(here)
        else:
            remote()

    def stage(a):
        for t in (1, 2, 3):
            y_send(a, t).wait_recv()
        total = ysum[a, y].astype(F32)
        for t in range(3):
            total = total + yrecv[a, t].astype(F32)
        tbuf[a] = total.astype(BF16).reshape(2, 32, WIDE)
        for d in range(2):
            def here():
                orecv[xh, a // 2, co] = tbuf[a, xh]

            o_each(a, d, lambda: o_send(a, d).start(), here)

    def g1():
        return copy(gw.at[:, 1 - co], g1recv, s_g.at[0], r_g.at[0], sibling)

    def g2():
        return copy(g2buf.at[:, 1 - xl], g2recv, s_g.at[1], r_g.at[1], dev(z, 1 - xl, co, xh, y))

    def g3(t):
        to = (z + t) % 8
        return copy(g3buf.at[to], g3recv.at[t - 1], s_g.at[1 + t], r_g.at[1 + t], dev(to, xl, co, xh, y))

    for s in range(4):
        second(s)
        core_send(s).start()
        if s:
            finish(s - 1)
    g1().start()
    finish(3)
    g1().wait_recv()
    g2buf[...] = (gw[:, co] + g1recv[...]).astype(BF16).reshape(8, 2, 16, 512)
    g2().start()
    finish(4)
    stage(0)
    for h in range(HEADS):
        dq_ref[:, h * 192 : (h + 1) * 192] = (dq_t[h] * SCALE).T[:, :192].astype(BF16)
    stage(1)
    g2().wait_recv()
    g3buf[...] = (g2buf[:, xl].astype(F32) + g2recv[...].astype(F32)).astype(BF16)
    for t in range(1, 8):
        g3(t).start()
    stage(2)
    stage(3)
    stage(4)
    for t in range(1, 8):
        g3(t).wait_recv()
    total = g3buf[z].astype(F32)
    for t in range(7):
        total = total + g3recv[t].astype(F32)
    gwo_ref[...] = total

    for d in range(2):
        for j in range(3):
            for c in range(2):
                def wait():
                    copy(tbuf.at[0, 0], orecv.at[(xh + d) % 2, j, c], s_o.at[0, 0],
                         r_o.at[(xh + d) % 2, j, c], sibling).wait_recv()

                if d == 0 and j == 1 and c == 0:
                    pl.when(co == 1)(wait)
                elif j == 2 and not (d == 0 and c == 1):
                    pl.when(co == 1)(wait)
                elif j < 2:
                    wait()
    total = orecv[0, 0].astype(F32)
    for k in range(1, 6):
        total = total + orecv[k // 3, k % 3].astype(F32)
    fin[...] = total.astype(BF16)

    def ag(t):
        to = (head + t) % 8
        return copy(fin, out_ref.at[:, y, xh], s_ag.at[t - 1], r_ag.at[t - 1], (ctx, to))

    for t in (2, 6, 1, 7, 3, 5, 4):
        ag(t).start()
    out_ref[:, y, xh] = fin[...]
    for t in range(1, 8):
        ag(t).wait_recv()

    full().wait_send()
    forward().wait_send()

    @pl.when(xl == 1)
    def _():
        piece().wait_send()
        for t in range(8):
            relay(t).wait_send()

    @pl.when(xl == 0)
    def _():
        half(0).wait_send()
        half(1).wait_send()

    for s in range(4):
        core_send(s).wait_send()
    for a in range(5):
        for t in (1, 2, 3):
            y_send(a, t).wait_send()
        for d in range(2):
            o_each(a, d, lambda: o_send(a, d).wait_send(), None)
    g1().wait_send()
    g2().wait_send()
    for t in range(1, 8):
        g3(t).wait_send()
        ag(t).wait_send()


def local(kv_latent, queries, grad_out, kv_up_weight, doc_ids):
    first_row = lax.axis_index("ctx") * ROWS
    docs = lax.dynamic_slice_in_dim(doc_ids, first_row, ROWS)
    marks = (docs[:, None] == jnp.arange(64, dtype=jnp.int32)[None, :]).astype(BF16)
    latx = jnp.concatenate([kv_latent, marks], axis=1)
    vm = pl.BlockSpec(memory_space=pltpu.VMEM)
    dma = pltpu.SemaphoreType.DMA
    V = pltpu.VMEM
    dq, out, gwo = pl.pallas_call(
        body,
        out_shape=(
            jax.ShapeDtypeStruct((ROWS, HEADS * (NOPE + ROPE)), BF16),
            jax.ShapeDtypeStruct((2, 4, 2, 32, WIDE), BF16),
            jax.ShapeDtypeStruct((16, 512), F32),
        ),
        in_specs=[vm] * 4,
        out_specs=(vm, vm, vm),
        scratch_shapes=[
            V((4, ROWS, 640), BF16), V((64, 640), BF16), V((2, ROWS, 256), BF16), V((2, 256, ROWS), BF16),
            V((2, 128, ROWS), BF16), V((512, 512), BF16), V((4, 512, ROWS), BF16), V((4, 2, 256, ROWS), BF16),
            V((4, 2, ROWS, ROWS), F32), V((4, 2, ROWS, ROWS), F32),
            V((2, 1, ROWS), F32), V((2, 1, ROWS), F32), V((2, 1, ROWS), F32), V((4, 2, 1, ROWS), F32),
            V((2, 256, ROWS), F32), V((16, 2, 16, 512), F32),
            V((5, 2, 256, WIDE), BF16), V((5, 256, WIDE), BF16), V((5, 4, 64, WIDE), BF16), V((5, 3, 64, WIDE), BF16),
            V((5, 2, 32, WIDE), BF16), V((2, 3, 2, 32, WIDE), BF16), V((2, 32, WIDE), BF16),
            V((16, 16, 512), F32), V((8, 2, 16, 512), BF16), V((8, 16, 512), BF16), V((8, 16, 512), BF16),
            V((7, 16, 512), BF16),
            dma((5,)), dma((8,)), dma((4,)), dma((5, 3)), dma((5, 2)), dma((7,)), dma((9,)),
            dma((4,)), dma((1,)), dma((5,)), dma((5, 3)), dma((2, 3, 2)), dma((7,)), dma((9,)),
        ],
        compiler_params=pltpu.CompilerParams(
            collective_id=0, has_side_effects=True, vmem_limit_bytes=56 * 1024 * 1024
        ),
        cost_estimate=pl.CostEstimate(flops=7_000_000_000, bytes_accessed=4_000_000, transcendentals=2_100_000),
    )(latx, queries, grad_out, kv_up_weight)
    return dq, out.reshape(ROWS, WIDE), gwo


def solution(mesh):
    return jax.shard_map(
        local,
        mesh=mesh,
        in_specs=(P("ctx", None), P("ctx", "head"), P("ctx", "head"), P(None, "head"), P()),
        out_specs=(P("ctx", "head"), P("ctx", None), P("ctx", "head")),
        check_vma=False,
    )
```

```python
import math

import jax
import jax.numpy as jnp
from jax import lax
from jax.experimental import pallas as pl
from jax.experimental.pallas import tpu as pltpu
from jax.sharding import PartitionSpec as P

NOPE, ROPE, VDIM, LATENT = 128, 64, 128, 512
ROWS = 512
HEADS = 2
BIG = 1e30
MESH = pl.DeviceIdType.MESH
SCALE = 1.0 / math.sqrt(NOPE + ROPE)
WIDE = LATENT + ROPE
MARKS = 32
KEY_ROWS = WIDE + MARKS
X_FIRST = (1, 3)
F32, BF16 = jnp.float32, jnp.bfloat16


def mm(a, b):
    return jnp.dot(a, b, preferred_element_type=F32)


def body(
    lat_hbm, q_hbm, do_hbm, w_hbm, docs_hbm, dq_ref, out_ref, gwo_ref,
    kbuf, relay_buf, zrecv, q, do, w, docs, qcat, q_t, do_t, w_t, kc, e_buf, g_buf, m_ref, l_ref, x_ref, mref,
    dq_acc, gw, sbuf, crecv, ysum, yrecv, xrecv, xsum, xyrecv, tbuf, orecv, fin, g1recv, g2buf, g2recv, g3buf, g3recv,
    s_in, s_p1, s_rel, s_fwd, s_z, s_core, s_x, s_y, s_o, s_ag, s_g,
    r_slot, r_rel, r_piece, r_half, r_z, r_core, r_x, r_y, r_o, r_ag, r_g,
):
    ctx = lax.axis_index("ctx")
    head = lax.axis_index("head")
    z, xl, co = ctx // 4, (ctx // 2) % 2, ctx % 2
    xh, y = head // 4, head % 4
    chip = ctx // 2

    def dev(z_, xl_, co_, xh_, y_):
        return (z_ * 4 + xl_ * 2 + co_, xh_ * 4 + y_)

    def copy(src, dst, ss, rs, to):
        return pltpu.make_async_remote_copy(
            src_ref=src, dst_ref=dst, send_sem=ss, recv_sem=rs, device_id=to, device_id_type=MESH
        )

    def lanes(k):
        return pl.ds(pl.multiple_of(k * 128, 128), 128)

    inputs = [
        pltpu.make_async_copy(docs_hbm.at[pl.ds(pl.multiple_of(chip * 8, 8), 8)], docs, s_in.at[0]),
        pltpu.make_async_copy(lat_hbm, kbuf.at[3, pl.ds(0, WIDE)], s_in.at[1]),
        pltpu.make_async_copy(w_hbm, w, s_in.at[2]),
        pltpu.make_async_copy(q_hbm, q, s_in.at[3]),
        pltpu.make_async_copy(do_hbm, do, s_in.at[4]),
    ]
    for c in inputs:
        c.start()

    barrier = pltpu.get_barrier_semaphore()
    partners = [(ctx, (head + t) % 8) for t in range(1, 8)]
    partners += [dev(z, 1 - xl, co, u // 4, u % 4) for u in range(8)]
    partners += [dev((z + t) % 8, xl, co, xh, y) for t in range(1, 8)]
    partners += [dev(z, xl, 1 - co, u, y) for u in range(2)]
    partners += [dev(z, 1 - xl, 1 - co, u, y) for u in range(2)]
    for dz in (1, 7):
        partners += [dev((z + dz) % 8, 1 - xl, k, u, y) for k in range(2) for u in range(2)]
        partners += [dev((z + dz) % 8, xl, 1 - co, u, y) for u in range(2)]
        partners += [dev((z + dz) % 8, xl, co, 1 - xh, y)]
    for to in partners:
        pl.semaphore_signal(barrier, inc=1, device_id=to, device_id_type=MESH)

    inputs[0].wait()
    mine = jnp.where(co == 0, docs[0:4, :], docs[4:8, :])
    mine = jnp.concatenate([mine[i : i + 1, :] for i in range(4)], axis=1)
    marks = (lax.broadcasted_iota(jnp.int32, (MARKS, ROWS), 0) == mine).astype(F32)
    kbuf[3, WIDE:, :] = marks.astype(BF16)
    inputs[1].wait()
    pl.semaphore_wait(barrier, len(partners))

    own = kbuf.at[3]
    sibling = dev(z, xl, 1 - co, xh, y)
    first = jnp.where(co == 1, 2, 0)
    direct = jnp.where(xl == 0, jnp.where(co == 0, 2, 0), 1)
    third = 3 - first - direct

    def full():
        slot = jnp.where(co == 0, 2, 0)
        return copy(own, kbuf.at[slot], s_p1.at[0], r_slot.at[slot], dev((z + co) % 8, xl, 1 - co, xh, y))

    def cut(ref, u):
        rows = pl.ds(pl.multiple_of((u // 4) * 304, 16), 304)
        return ref.at[rows, lanes(u % 4)]

    def piece():
        return copy(cut(own, head), relay_buf, s_p1.at[1], r_rel.at[0], dev((z + 1) % 8, 1, 1 - co, xh, y))

    def half(d):
        cols = pl.ds(d * 256, 256)
        return copy(
            own.at[:, cols], kbuf.at[1, :, cols], s_p1.at[2 + d], r_half.at[d], dev(z, 1, co, (xh + d) % 2, y)
        )

    def relay(t):
        slot = jnp.where(co == 0, 2, 0)
        return copy(
            relay_buf, cut(kbuf.at[slot], head), s_rel.at[t], r_piece.at[t], (z * 4 + co, (head + t) % 8)
        )

    def got_piece(t):
        part = cut(kbuf.at[direct], (head + 8 - t) % 8)
        return copy(part, part, s_rel.at[t], r_piece.at[t], sibling)

    def pass_piece(t):
        u = (head + 8 - t) % 8
        return copy(cut(kbuf.at[direct], u), cut(kbuf.at[1], u), s_fwd.at[t], r_slot.at[1], sibling)

    def pass_half(d):
        cols = pl.ds(d * 256, 256)
        slot = jnp.where(co == 0, 0, 2)
        return copy(kbuf.at[1, :, cols], kbuf.at[slot, :, cols], s_fwd.at[d], r_slot.at[slot], sibling)

    late = (xl == 1) & (co == 1)

    @pl.when(xl == 1)
    def _():
        piece().start()

    @pl.when(jnp.logical_not(late))
    def _():
        full().start()

    @pl.when(xl == 0)
    def _():
        half(0).start()
        half(1).start()

    def wait_slot(s):
        copy(own, kbuf.at[s], s_p1.at[0], r_slot.at[s], sibling).wait_recv()

    for c in inputs[2:]:
        c.wait()
    w_t[...] = w[...].T
    query_mask = ((marks.T - 1.0) * BIG).astype(BF16)
    for h in range(HEADS):
        qh = q[:, h * (NOPE + ROPE) : (h + 1) * (NOPE + ROPE)]
        qcat[h] = jnp.concatenate([qh, query_mask], axis=1)
        q_t[h] = qh.T
        do_t[h] = do[:, h * VDIM : (h + 1) * VDIM].T

    @pl.when(late)
    def _():
        piece().wait_send()
        full().start()

    def stream(s, diagonal):
        tail = kbuf[s, LATENT:, :]
        kv = mm(w_t[...], kbuf[s, :LATENT, :]).astype(BF16)
        for h in range(HEADS):
            base = h * (NOPE + VDIM)
            keys = jnp.concatenate([kv[base : base + NOPE], tail], axis=0)
            kc[s, h] = keys[: NOPE + ROPE].T
            scores = mm(qcat[h], keys) * (SCALE * math.log2(math.e))
            if diagonal:
                query = lax.broadcasted_iota(jnp.int32, (ROWS, ROWS), 0)
                key = lax.broadcasted_iota(jnp.int32, (ROWS, ROWS), 1)
                scores = jnp.where(key <= query, scores, -BIG)
            top = jnp.max(scores, axis=1, keepdims=True)
            if not diagonal:
                top = jnp.maximum(top, m_ref[h])
            e = jnp.exp2(scores - top)
            g = mm(do[:, h * VDIM : (h + 1) * VDIM], kv[base + NOPE : base + NOPE + VDIM])
            mass = jnp.sum(e, axis=1, keepdims=True)
            cross = jnp.sum(e * g, axis=1, keepdims=True)
            if not diagonal:
                factor = jnp.exp2(m_ref[h] - top)
                mass = mass + l_ref[h] * factor
                cross = cross + x_ref[h] * factor
            m_ref[h] = top
            l_ref[h] = mass
            x_ref[h] = cross
            mref[s, h] = top
            e_buf[s, h] = e
            g_buf[s, h] = g

    @pl.when(xl == 1)
    def _():
        piece().wait_recv()
        for t in (2, 6, 1, 3, 5, 7, 4, 0):
            relay(t).start()

    stream(3, True)
    wait_slot(first)
    stream(first, False)

    @pl.when(xl == 0)
    def _():
        for t in (0, 4, 1, 3, 5, 7, 2, 6):
            got_piece(t).wait_recv()
            pass_piece(t).start()

    @pl.when(xl == 1)
    def _():
        for d in range(2):
            half(d).wait_recv()
            pass_half(d).start()

    stream(direct, False)
    wait_slot(third)
    stream(third, False)

    @pl.when(co == 0)
    def _():
        sbuf[4, 0] = jnp.zeros((2, 144, 512), BF16)

    @pl.when(co == 1)
    def _():
        crecv[4] = jnp.zeros((2, 144, 512), BF16)

    def second(i):
        s = jnp.where(co == 0, (0, 1, 3, 2)[i], (0, 2, 1, 3)[i])
        grad_rope = None
        parts = []
        for h in range(HEADS):
            inverse = 1.0 / l_ref[h]
            delta = x_ref[h] * inverse
            p = e_buf[s, h] * (jnp.exp2(mref[s, h] - m_ref[h]) * inverse)
            ds = (p * (g_buf[s, h] - delta)).astype(BF16)
            pb = p.astype(BF16)
            grad_q = mm(ds, kc[s, h])
            if i == 0:
                dq_acc[h] = grad_q
            else:
                dq_acc[h] += grad_q
            grad_k = mm(q_t[h], ds) * SCALE
            grad_v = mm(do_t[h], pb)
            parts += [grad_k[:NOPE], grad_v]
            rope = grad_k[NOPE:]
            grad_rope = rope if grad_rope is None else grad_rope + rope
        dkv = jnp.concatenate(parts, axis=0).astype(BF16)
        grad = jnp.concatenate([mm(w[...], dkv), grad_rope], axis=0)
        sbuf[s + co] = grad.astype(BF16).reshape(2, 2, 144, 512)
        part = lax.dot_general(
            kbuf[s, :LATENT, :], dkv, (((1,), (1,)), ((), ())), preferred_element_type=F32
        ).reshape(16, 2, 16, 512)
        if i == 0:
            gw[...] = part
        else:
            gw[...] += part

    def core_send(i):
        a = jnp.where(co == 0, (0, 1, 3, 2)[i], (1, 3, 2, 4)[i])
        return copy(sbuf.at[a, 1 - co], crecv.at[a], s_core.at[i], r_core.at[a], sibling)

    def z_send(c):
        return copy(sbuf.at[0, c], zrecv, s_z.at[c], r_z.at[0], dev((z + 7) % 8, xl, c, xh, y))

    def x_send(a):
        return copy(ysum.at[a, 1 - xh], xrecv.at[a], s_x.at[a], r_x.at[a], dev(z, xl, co, 1 - xh, y))

    def y_send(a, t):
        to = (y + t) % 4
        if a in X_FIRST:
            src, dst = xsum.at[a, :, lanes(to)], xyrecv.at[a, t - 1]
        else:
            src, dst = ysum.at[a, :, :, lanes(to)], yrecv.at[a, t - 1]
        return copy(src, dst, s_y.at[a, t - 1], r_y.at[a, t - 1], dev(z, xl, co, xh, to))

    def finish(a):
        def wait():
            copy(sbuf.at[a, 0], crecv.at[a], s_core.at[0], r_core.at[a], sibling).wait_recv()

        total = sbuf[a, co].astype(F32)
        if a == 4:
            pl.when(co == 0)(wait)
            z_send(0).wait_recv()
            total = total + zrecv[...].astype(F32)
        else:
            wait()
        ysum[a] = (total + crecv[a].astype(F32)).astype(BF16)
        if a in X_FIRST:
            x_send(a).start()
        else:
            for t in (2, 1, 3):
                y_send(a, t).start()

    def middle(a):
        x_send(a).wait_recv()
        xsum[a] = (ysum[a, xh].astype(F32) + xrecv[a].astype(F32)).astype(BF16)
        for t in (2, 1, 3):
            y_send(a, t).start()

    def o_send(a, d):
        owner = (2 * chip + 29 + a) % 32
        to = (xh + d) % 2
        src = tbuf.at[a, 0] if a in X_FIRST else tbuf.at[a, to]
        k = (0, 0, 0, 1, 2)[a] + d
        return copy(src, orecv.at[k, co], s_o.at[a, d], r_o.at[k, co], (owner, to * 4 + y))

    def o_each(a, remote, here):
        if a >= 3:
            pl.when(co != a - 3)(lambda: remote(0))
            if here is not None:
                pl.when(co == a - 3)(here)
        else:
            remote(0)
        if a not in X_FIRST:
            remote(1)

    def stage(a):
        for t in (1, 2, 3):
            y_send(a, t).wait_recv()
        if a in X_FIRST:
            total = xsum[a, :, lanes(y)].astype(F32)
            for t in range(3):
                total = total + xyrecv[a, t].astype(F32)
            tbuf[a, 0] = total.astype(BF16)
        else:
            total = ysum[a, :, :, lanes(y)].astype(F32)
            for t in range(3):
                total = total + yrecv[a, t].astype(F32)
            tbuf[a] = total.astype(BF16)

        def here():
            orecv[(0, 0, 0, 1, 2)[a], co] = tbuf[a, 0] if a in X_FIRST else tbuf[a, xh]

        o_each(a, lambda d: o_send(a, d).start(), here)

    def g1():
        return copy(gw.at[:, 1 - co], g1recv, s_g.at[0], r_g.at[0], sibling)

    def g2():
        return copy(g2buf.at[:, 1 - xl], g2recv, s_g.at[1], r_g.at[1], dev(z, 1 - xl, co, xh, y))

    def g3(t):
        to = (z + t) % 8
        return copy(g3buf.at[to], g3recv.at[t - 1], s_g.at[1 + t], r_g.at[1 + t], dev(to, xl, co, xh, y))

    def arrived(k, c):
        copy(tbuf.at[0, 0], orecv.at[k, c], s_o.at[0, 0], r_o.at[k, c], sibling).wait_recv()

    def ag(t):
        return copy(
            fin, out_ref.at[:, xh, :, lanes(y)], s_ag.at[t - 1], r_ag.at[t - 1], (ctx, (head + t) % 8)
        )

    def final(parts):
        for k, c in parts:
            arrived(k, c)
        total = orecv[0].astype(F32)
        for k in range(1, 2 if len(parts) == 3 else 4):
            total = total + orecv[k].astype(F32)
        fin[...] = total.astype(BF16)
        for t in (2, 6, 1, 7, 3, 5, 4):
            ag(t).start()
        out_ref[:, xh, :, lanes(y)] = fin[...]

    second(0)

    @pl.when(co == 0)
    def _():
        z_send(0).start()
        z_send(1).start()

    @pl.when(co == 1)
    def _():
        core_send(0).start()

    second(1)
    core_send(1).start()
    finish(1)
    second(2)
    core_send(2).start()
    finish(3)
    second(3)
    core_send(3).start()
    g1().start()
    finish(2)
    middle(1)
    g1().wait_recv()
    g2buf[...] = (gw[:, co] + g1recv[...]).astype(BF16).reshape(8, 2, 16, 512)
    g2().start()
    finish(4)
    middle(3)
    g2().wait_recv()
    g3buf[...] = (g2buf[:, xl].astype(F32) + g2recv[...].astype(F32)).astype(BF16)
    for t in range(1, 8):
        g3(t).start()
    stage(2)
    stage(1)
    stage(3)
    stage(4)

    @pl.when(co == 0)
    def _():
        final([(0, 0), (0, 1), (1, 1)])

    @pl.when(co == 1)
    def _():
        final([(0, 0), (0, 1), (1, 0), (1, 1), (2, 0), (3, 0), (3, 1)])

    for h in range(HEADS):
        dq_ref[:, h * 192 : (h + 1) * 192] = (dq_acc[h] * SCALE).astype(BF16)
    for t in range(1, 8):
        g3(t).wait_recv()
    total = g3buf[z].astype(F32)
    for t in range(7):
        total = total + g3recv[t].astype(F32)
    gwo_ref[...] = total
    for t in range(1, 8):
        ag(t).wait_recv()

    full().wait_send()
    pl.when((xl == 1) & (co == 0))(lambda: piece().wait_send())

    @pl.when(xl == 1)
    def _():
        for t in range(8):
            relay(t).wait_send()
        for d in range(2):
            pass_half(d).wait_send()

    @pl.when(xl == 0)
    def _():
        half(0).wait_send()
        half(1).wait_send()
        for t in range(8):
            pass_piece(t).wait_send()

    @pl.when(co == 0)
    def _():
        z_send(0).wait_send()
        z_send(1).wait_send()

    @pl.when(co == 1)
    def _():
        core_send(0).wait_send()

    for i in range(1, 4):
        core_send(i).wait_send()
    for a in range(1, 5):
        if a in X_FIRST:
            x_send(a).wait_send()
        for t in (1, 2, 3):
            y_send(a, t).wait_send()
        o_each(a, lambda d: o_send(a, d).wait_send(), None)
    g1().wait_send()
    g2().wait_send()
    for t in range(1, 8):
        g3(t).wait_send()
        ag(t).wait_send()


def place(dq, out, gwo, dq_ref, out_ref, gwo_ref, dq_v, out_v, gwo_v, sem):
    held = ((dq, dq_v, dq_ref), (out, out_v, out_ref), (gwo, gwo_v, gwo_ref))
    come = [pltpu.make_async_copy(a, b, sem.at[0, i]) for i, (a, b, _) in enumerate(held)]
    go = [pltpu.make_async_copy(b, c, sem.at[1, i]) for i, (_, b, c) in enumerate(held)]
    for c in come:
        c.start()
    for i in range(3):
        come[i].wait()
        go[i].start()
    for c in go:
        c.wait()


def local(kv_latent, queries, grad_out, kv_up_weight, doc_ids):
    vm = pl.BlockSpec(memory_space=pltpu.VMEM)
    hbm = pl.BlockSpec(memory_space=pl.ANY)
    dma = pltpu.SemaphoreType.DMA
    V = pltpu.VMEM
    dq, out, gwo = pl.pallas_call(
        body,
        out_shape=(
            jax.ShapeDtypeStruct((ROWS, HEADS * (NOPE + ROPE)), BF16),
            jax.ShapeDtypeStruct((2, 2, 144, ROWS), BF16),
            jax.ShapeDtypeStruct((16, 512), F32),
        ),
        in_specs=[hbm] * 5,
        out_specs=(vm, vm, vm),
        scratch_shapes=[
            V((4, KEY_ROWS, ROWS), BF16), V((304, 128), BF16), V((2, 144, ROWS), BF16),
            V((ROWS, 384), BF16), V((ROWS, 256), BF16), V((512, 512), BF16), V((8, 128), jnp.int32),
            V((2, ROWS, NOPE + ROPE + MARKS), BF16), V((2, 192, ROWS), BF16), V((2, 128, ROWS), BF16), V((512, 512), BF16),
            V((4, 2, ROWS, 192), BF16), V((4, 2, ROWS, ROWS), F32), V((4, 2, ROWS, ROWS), F32),
            V((2, ROWS, 1), F32), V((2, ROWS, 1), F32), V((2, ROWS, 1), F32), V((4, 2, ROWS, 1), F32),
            V((2, ROWS, 192), F32), V((16, 2, 16, 512), F32),
            V((5, 2, 2, 144, 512), BF16), V((5, 2, 144, 512), BF16), V((5, 2, 144, 512), BF16),
            V((5, 3, 2, 144, 128), BF16), V((5, 144, 512), BF16), V((5, 144, 512), BF16), V((5, 3, 144, 128), BF16),
            V((5, 2, 144, 128), BF16), V((4, 2, 144, 128), BF16), V((2, 144, 128), BF16),
            V((16, 16, 512), F32), V((8, 2, 16, 512), BF16), V((8, 16, 512), BF16), V((8, 16, 512), BF16),
            V((7, 16, 512), BF16),
            dma((5,)), dma((4,)), dma((8,)), dma((8,)), dma((2,)), dma((4,)), dma((5,)), dma((5, 3)), dma((5, 2)), dma((7,)),
            dma((9,)),
            dma((3,)), dma((1,)), dma((8,)), dma((2,)), dma((1,)), dma((5,)), dma((5,)), dma((5, 3)), dma((5, 2)), dma((7,)),
            dma((9,)),
        ],
        compiler_params=pltpu.CompilerParams(
            collective_id=0, has_side_effects=True, vmem_limit_bytes=58 * 1024 * 1024
        ),
        cost_estimate=pl.CostEstimate(flops=7_000_000_000, bytes_accessed=4_000_000, transcendentals=2_100_000),
    )(kv_latent.T, queries, grad_out, kv_up_weight, doc_ids.reshape(128, 128))
    dq, out, gwo = pl.pallas_call(
        place,
        out_shape=(
            jax.ShapeDtypeStruct((ROWS, HEADS * (NOPE + ROPE)), BF16),
            jax.ShapeDtypeStruct((WIDE, ROWS), BF16),
            jax.ShapeDtypeStruct((16, 512), F32),
        ),
        in_specs=[hbm] * 3,
        out_specs=(hbm, hbm, hbm),
        scratch_shapes=[V((ROWS, 384), BF16), V((WIDE, ROWS), BF16), V((16, 512), F32), dma((2, 3))],
    )(dq, out.reshape(WIDE, ROWS), gwo)
    return dq, out.T, gwo


def solution(mesh):
    return jax.shard_map(
        local,
        mesh=mesh,
        in_specs=(P("ctx", None), P("ctx", "head"), P("ctx", "head"), P(None, "head"), P()),
        out_specs=(P("ctx", "head"), P("ctx", None), P("ctx", "head")),
        check_vma=False,
    )
```

```python
import math

import jax
import jax.numpy as jnp
from jax import lax
from jax.experimental import pallas as pl
from jax.experimental.pallas import tpu as pltpu
from jax.sharding import PartitionSpec as P

NOPE, ROPE, VDIM, LATENT = 128, 64, 128, 512
ROWS = 512
HEADS = 2
BIG = 1e30
MESH = pl.DeviceIdType.MESH
SCALE = 1.0 / math.sqrt(NOPE + ROPE)
WIDE = LATENT + ROPE
MARKS = 32
KEY_ROWS = WIDE + MARKS
X_FIRST = (2,)
FIRST_PART = (0, 0, 0, 2, 1)
F32, BF16 = jnp.float32, jnp.bfloat16


def mm(a, b):
    return jnp.dot(a, b, preferred_element_type=F32)


def body(
    lat_hbm, q_hbm, do_hbm, w_hbm, docs_hbm, dq_ref, out_ref, gwo_ref,
    kbuf, relay_buf, zrecv, q, do, w, docs, qcat, q_t, do_t, w_t, kc, e_buf, g_buf, m_ref, l_ref, x_ref, mref,
    dq_acc, gw, sbuf, crecv, ysum, yrecv, xrecv, xsum, xyrecv, tbuf, orecv, fin, g1recv, g2buf, g2recv, g3buf, g3recv,
    s_in, s_p1, s_rel, s_fwd, s_z, s_core, s_x, s_y, s_o, s_ag, s_g,
    r_slot, r_rel, told, r_piece, r_half, r_z, r_core, r_x, r_y, r_o, r_ag, r_g,
):
    ctx = lax.axis_index("ctx")
    head = lax.axis_index("head")
    z, xl, co = ctx // 4, (ctx // 2) % 2, ctx % 2
    xh, y = head // 4, head % 4
    chip = ctx // 2

    def dev(z_, xl_, co_, xh_, y_):
        return (z_ * 4 + xl_ * 2 + co_, xh_ * 4 + y_)

    def copy(src, dst, ss, rs, to):
        return pltpu.make_async_remote_copy(
            src_ref=src, dst_ref=dst, send_sem=ss, recv_sem=rs, device_id=to, device_id_type=MESH
        )

    def lanes(k):
        return pl.ds(pl.multiple_of(k * 128, 128), 128)

    barrier = pltpu.get_barrier_semaphore()
    partners = [(ctx, (head + t) % 8) for t in range(1, 8)]
    partners += [dev(z, 1 - xl, co, u // 4, u % 4) for u in range(8)]
    partners += [dev(z, xl, 1 - co, u, y) for u in range(2)]
    partners += [dev(z, 1 - xl, 1 - co, u, y) for u in range(2)]
    below, above = z > 0, z < 7
    beside = jnp.where(xl == 0, below, above)

    def greet(to):
        pl.semaphore_signal(barrier, inc=1, device_id=to, device_id_type=MESH)

    for to in partners:
        greet(to)

    @pl.when(below)
    def _():
        for k in range(2):
            greet(dev(z - 1, xl, k, xh, y))

    @pl.when(above)
    def _():
        for k in range(2):
            greet(dev(z + 1, xl, k, xh, y))

    @pl.when(beside)
    def _():
        for k in range(2):
            for u in range(2):
                greet(dev(z - 1 + 2 * xl, 1 - xl, k, u, y))

    greetings = (
        len(partners) + jnp.where(below, 2, 0) + jnp.where(above, 2, 0) + jnp.where(beside, 4, 0)
    )

    inputs = [
        pltpu.make_async_copy(docs_hbm.at[pl.ds(pl.multiple_of(chip * 8, 8), 8)], docs, s_in.at[0]),
        pltpu.make_async_copy(lat_hbm, kbuf.at[3, pl.ds(0, WIDE)], s_in.at[1]),
        pltpu.make_async_copy(w_hbm, w, s_in.at[2]),
        pltpu.make_async_copy(q_hbm, q, s_in.at[3]),
        pltpu.make_async_copy(do_hbm, do, s_in.at[4]),
    ]
    for c in inputs:
        c.start()

    inputs[0].wait()
    mine = jnp.where(co == 0, docs[0:4, :], docs[4:8, :])
    mine = jnp.concatenate([mine[i : i + 1, :] for i in range(4)], axis=1)
    marks = (lax.broadcasted_iota(jnp.int32, (MARKS, ROWS), 0) == mine).astype(F32)
    kbuf[3, WIDE:, :] = marks.astype(BF16)
    inputs[1].wait()
    pl.semaphore_wait(barrier, greetings)

    def tell(k):
        @pl.when(z >= 2**k)
        def _():
            pl.semaphore_signal(told.at[k], inc=1, device_id=dev(z - 2**k, xl, co, xh, y), device_id_type=MESH)

        @pl.when(z + 2**k < 8)
        def _():
            pl.semaphore_signal(told.at[k], inc=1, device_id=dev(z + 2**k, xl, co, xh, y), device_id_type=MESH)

    def hear(k):
        pl.semaphore_wait(told.at[k], jnp.where(z >= 2**k, 1, 0) + jnp.where(z + 2**k < 8, 1, 0))

    tell(0)

    for s in range(3):
        @pl.when((z == 0) & (s < 3 - 2 * xl - co))
        def _():
            kbuf[s, :WIDE, :] = jnp.zeros((WIDE, ROWS), BF16)
            kbuf[s, WIDE:, :] = jnp.ones((MARKS, ROWS), BF16)

    @pl.when(z == 7)
    def _():
        zrecv[...] = jnp.zeros((2, 144, ROWS), BF16)

    @pl.when(chip == 15)
    def _():
        orecv[0:2] = jnp.zeros((2, 2, 144, 128), BF16)

    own = kbuf.at[3]
    sibling = dev(z, xl, 1 - co, xh, y)
    first = jnp.where(co == 1, 2, 0)
    direct = jnp.where(xl == 0, jnp.where(co == 0, 2, 0), 1)
    third = 3 - first - direct

    def full():
        slot = jnp.where(co == 0, 2, 0)
        return copy(own, kbuf.at[slot], s_p1.at[0], r_slot.at[slot], dev((z + co) % 8, xl, 1 - co, xh, y))

    def cut(ref, u):
        rows = pl.ds(pl.multiple_of((u // 4) * 304, 16), 304)
        return ref.at[rows, lanes(u % 4)]

    def piece():
        return copy(cut(own, head), relay_buf, s_p1.at[1], r_rel.at[0], dev((z + 1) % 8, 1, 1 - co, xh, y))

    def half(d):
        cols = pl.ds(d * 256, 256)
        return copy(
            own.at[:, cols], kbuf.at[1, :, cols], s_p1.at[2 + d], r_half.at[d], dev(z, 1, co, (xh + d) % 2, y)
        )

    def relay(t):
        slot = jnp.where(co == 0, 2, 0)
        return copy(
            relay_buf, cut(kbuf.at[slot], head), s_rel.at[t], r_piece.at[t], (z * 4 + co, (head + t) % 8)
        )

    def got_piece(t):
        part = cut(kbuf.at[direct], (head + 8 - t) % 8)
        return copy(part, part, s_rel.at[t], r_piece.at[t], sibling)

    def pass_piece(t):
        u = (head + 8 - t) % 8
        return copy(cut(kbuf.at[direct], u), cut(kbuf.at[1], u), s_fwd.at[t], r_slot.at[1], sibling)

    def pass_half(d):
        cols = pl.ds(d * 256, 256)
        slot = jnp.where(co == 0, 0, 2)
        return copy(kbuf.at[1, :, cols], kbuf.at[slot, :, cols], s_fwd.at[d], r_slot.at[slot], sibling)

    late = (xl == 1) & (co == 1)
    sends_full = (co == 0) | above

    @pl.when((xl == 1) & above)
    def _():
        piece().start()

    @pl.when(jnp.logical_not(late) & sends_full)
    def _():
        full().start()

    @pl.when(xl == 0)
    def _():
        half(0).start()
        half(1).start()

    def wait_slot(s):
        copy(own, kbuf.at[s], s_p1.at[0], r_slot.at[s], sibling).wait_recv()

    for c in inputs[2:]:
        c.wait()
    w_t[...] = w[...].T
    query_mask = ((marks.T - 1.0) * BIG).astype(BF16)
    for h in range(HEADS):
        qh = q[:, h * (NOPE + ROPE) : (h + 1) * (NOPE + ROPE)]
        qcat[h] = jnp.concatenate([qh, query_mask], axis=1)
        q_t[h] = qh.T
        do_t[h] = do[:, h * VDIM : (h + 1) * VDIM].T

    @pl.when(late & above)
    def _():
        piece().wait_send()
        full().start()

    def stream(s, diagonal):
        tail = kbuf[s, LATENT:, :]
        kv = mm(w_t[...], kbuf[s, :LATENT, :]).astype(BF16)
        for h in range(HEADS):
            base = h * (NOPE + VDIM)
            keys = jnp.concatenate([kv[base : base + NOPE], tail], axis=0)
            kc[s, h] = keys[: NOPE + ROPE].T
            scores = mm(qcat[h], keys) * (SCALE * math.log2(math.e))
            if diagonal:
                query = lax.broadcasted_iota(jnp.int32, (ROWS, ROWS), 0)
                key = lax.broadcasted_iota(jnp.int32, (ROWS, ROWS), 1)
                scores = jnp.where(key <= query, scores, -BIG)
            top = jnp.max(scores, axis=1, keepdims=True)
            if not diagonal:
                top = jnp.maximum(top, m_ref[h])
            e = jnp.exp2(scores - top)
            g = mm(do[:, h * VDIM : (h + 1) * VDIM], kv[base + NOPE : base + NOPE + VDIM])
            mass = jnp.sum(e, axis=1, keepdims=True)
            cross = jnp.sum(e * g, axis=1, keepdims=True)
            if not diagonal:
                factor = jnp.exp2(m_ref[h] - top)
                mass = mass + l_ref[h] * factor
                cross = cross + x_ref[h] * factor
            m_ref[h] = top
            l_ref[h] = mass
            x_ref[h] = cross
            mref[s, h] = top
            e_buf[s, h] = e
            g_buf[s, h] = g

    @pl.when((xl == 1) & below)
    def _():
        piece().wait_recv()
        for t in (2, 6, 1, 3, 5, 7, 4, 0):
            relay(t).start()

    stream(3, True)
    hear(0)
    tell(1)
    pl.when((co == 1) | below)(lambda: wait_slot(first))
    stream(first, False)

    @pl.when((xl == 0) & below)
    def _():
        for t in (0, 4, 1, 3, 5, 7, 2, 6):
            got_piece(t).wait_recv()
            pass_piece(t).start()

    @pl.when(xl == 1)
    def _():
        for d in range(2):
            half(d).wait_recv()
            pass_half(d).start()

    stream(direct, False)
    pl.when((xl == 1) | below)(lambda: wait_slot(third))
    stream(third, False)

    @pl.when(co == 0)
    def _():
        sbuf[4, 0] = jnp.zeros((2, 144, 512), BF16)

    @pl.when(co == 1)
    def _():
        crecv[4] = jnp.zeros((2, 144, 512), BF16)

    def second(i, meanwhile=None):
        s = jnp.where(co == 0, (0, 1, 3, 2)[i], (3, 0, 2, 1)[i])
        grad_rope = None
        parts = []
        for h in range(HEADS):
            inverse = 1.0 / l_ref[h]
            delta = x_ref[h] * inverse
            p = e_buf[s, h] * (jnp.exp2(mref[s, h] - m_ref[h]) * inverse)
            ds = (p * (g_buf[s, h] - delta)).astype(BF16)
            pb = p.astype(BF16)
            grad_q = mm(ds, kc[s, h])
            if i == 0:
                dq_acc[h] = grad_q
            else:
                dq_acc[h] += grad_q
            grad_k = mm(q_t[h], ds) * SCALE
            grad_v = mm(do_t[h], pb)
            parts += [grad_k[:NOPE], grad_v]
            rope = grad_k[NOPE:]
            grad_rope = rope if grad_rope is None else grad_rope + rope
        dkv = jnp.concatenate(parts, axis=0).astype(BF16)
        if meanwhile is not None:
            meanwhile()
        grad = jnp.concatenate([mm(w[...], dkv), grad_rope], axis=0)
        sbuf[s + co] = grad.astype(BF16).reshape(2, 2, 144, 512)
        part = lax.dot_general(
            kbuf[s, :LATENT, :], dkv, (((1,), (1,)), ((), ())), preferred_element_type=F32
        ).reshape(16, 2, 16, 512)
        if i == 0:
            gw[...] = part
        else:
            gw[...] += part

    def core_send(i):
        a = jnp.where(co == 0, (0, 1, 3, 2)[i], (4, 1, 3, 2)[i])
        return copy(sbuf.at[a, 1 - co], crecv.at[a], s_core.at[i], r_core.at[a], sibling)

    def z_send(c):
        return copy(sbuf.at[0, c], zrecv, s_z.at[c], r_z.at[0], dev((z + 7) % 8, xl, c, xh, y))

    def x_send(a):
        return copy(ysum.at[a, 1 - xh], xrecv.at[a], s_x.at[a], r_x.at[a], dev(z, xl, co, 1 - xh, y))

    def y_send(a, t):
        to = (y + t) % 4
        if a in X_FIRST:
            src, dst = xsum.at[a, :, lanes(to)], xyrecv.at[a, t - 1]
        else:
            src, dst = ysum.at[a, :, :, lanes(to)], yrecv.at[a, t - 1]
        return copy(src, dst, s_y.at[a, t - 1], r_y.at[a, t - 1], dev(z, xl, co, xh, to))

    def finish(a):
        def wait():
            copy(sbuf.at[a, 0], crecv.at[a], s_core.at[0], r_core.at[a], sibling).wait_recv()

        total = sbuf[a, co].astype(F32)
        if a == 4:
            pl.when(co == 0)(wait)
            pl.when(above)(lambda: z_send(0).wait_recv())
            total = total + zrecv[...].astype(F32)
        else:
            wait()
        ysum[a] = (total + crecv[a].astype(F32)).astype(BF16)
        if a in X_FIRST:
            x_send(a).start()
        else:
            for t in (2, 1, 3):
                y_send(a, t).start()

    def middle(a):
        x_send(a).wait_recv()
        xsum[a] = (ysum[a, xh].astype(F32) + xrecv[a].astype(F32)).astype(BF16)
        for t in (2, 1, 3):
            y_send(a, t).start()

    def o_send(a, d):
        owner = (2 * chip + 29 + a) % 32
        to = (xh + d) % 2
        src = tbuf.at[a, 0] if a in X_FIRST else tbuf.at[a, to]
        k = FIRST_PART[a] + d
        return copy(src, orecv.at[k, co], s_o.at[a, d], r_o.at[k, co], (owner, to * 4 + y))

    def o_each(a, remote, here):
        def both():
            remote(0)
            if a not in X_FIRST:
                remote(1)

        if a < 3:
            pl.when(chip > 0)(both)
        else:
            pl.when(co != a - 3)(lambda: remote(0))
            if here is not None:
                pl.when(co == a - 3)(here)
            remote(1)

    def stage(a):
        for t in (1, 2, 3):
            y_send(a, t).wait_recv()
        if a in X_FIRST:
            total = xsum[a, :, lanes(y)].astype(F32)
            for t in range(3):
                total = total + xyrecv[a, t].astype(F32)
            tbuf[a, 0] = total.astype(BF16)
        else:
            total = ysum[a, :, :, lanes(y)].astype(F32)
            for t in range(3):
                total = total + yrecv[a, t].astype(F32)
            tbuf[a] = total.astype(BF16)

        def here():
            orecv[FIRST_PART[a], co] = tbuf[a, 0] if a in X_FIRST else tbuf[a, xh]

        o_each(a, lambda d: o_send(a, d).start(), here)

    def g1():
        return copy(gw.at[:, 1 - co], g1recv, s_g.at[0], r_g.at[0], sibling)

    def g2():
        return copy(g2buf.at[:, 1 - xl], g2recv, s_g.at[1], r_g.at[1], dev(z, 1 - xl, co, xh, y))

    def g3(t):
        to = (z + t) % 8
        return copy(g3buf.at[to], g3recv.at[t - 1], s_g.at[1 + t], r_g.at[1 + t], dev(to, xl, co, xh, y))

    def arrived(k, c):
        copy(tbuf.at[0, 0], orecv.at[k, c], s_o.at[0, 0], r_o.at[k, c], sibling).wait_recv()

    def ag(t):
        return copy(
            fin, out_ref.at[:, xh, :, lanes(y)], s_ag.at[t - 1], r_ag.at[t - 1], (ctx, (head + t) % 8)
        )

    def final(count, parts):
        @pl.when(chip < 15)
        def _():
            for k, c in parts[0]:
                arrived(k, c)

        for k, c in parts[1]:
            arrived(k, c)
        total = orecv[0].astype(F32)
        for k in range(1, count):
            total = total + orecv[k].astype(F32)
        fin[...] = total.astype(BF16)
        for t in (2, 6, 1, 7, 3, 5, 4):
            ag(t).start()
        out_ref[:, xh, :, lanes(y)] = fin[...]

    second(0)

    hear(1)
    tell(2)

    @pl.when((co == 0) & below)
    def _():
        z_send(0).start()
        z_send(1).start()

    @pl.when(co == 1)
    def _():
        core_send(0).start()

    second(1)
    core_send(1).start()
    second(2, lambda: finish(1))
    core_send(2).start()
    second(3, lambda: finish(3))
    core_send(3).start()
    g1().start()
    finish(2)
    g1().wait_recv()
    g2buf[...] = (gw[:, co] + g1recv[...]).astype(BF16).reshape(8, 2, 16, 512)
    g2().start()
    stage(1)
    finish(4)
    stage(3)
    g2().wait_recv()
    g3buf[...] = (g2buf[:, xl].astype(F32) + g2recv[...].astype(F32)).astype(BF16)
    hear(2)
    for t in range(1, 8):
        g3(t).start()
    middle(2)

    stage(4)
    stage(2)

    @pl.when(co == 0)
    def _():
        final(4, ([(0, 0), (0, 1), (1, 0), (1, 1)], [(2, 1), (3, 0), (3, 1)]))

    @pl.when(co == 1)
    def _():
        final(3, ([(0, 0), (0, 1)], [(1, 0), (2, 0), (2, 1)]))

    for h in range(HEADS):
        dq_ref[:, h * 192 : (h + 1) * 192] = (dq_acc[h] * SCALE).astype(BF16)
    for t in range(1, 8):
        g3(t).wait_recv()
    total = g3buf[z].astype(F32)
    for t in range(7):
        total = total + g3recv[t].astype(F32)
    gwo_ref[...] = total
    for t in range(1, 8):
        ag(t).wait_recv()

    pl.when(sends_full)(lambda: full().wait_send())
    pl.when((xl == 1) & (co == 0) & above)(lambda: piece().wait_send())

    @pl.when((xl == 1) & below)
    def _():
        for t in range(8):
            relay(t).wait_send()

    @pl.when(xl == 1)
    def _():
        for d in range(2):
            pass_half(d).wait_send()

    @pl.when(xl == 0)
    def _():
        half(0).wait_send()
        half(1).wait_send()

    @pl.when((xl == 0) & below)
    def _():
        for t in range(8):
            pass_piece(t).wait_send()

    @pl.when((co == 0) & below)
    def _():
        z_send(0).wait_send()
        z_send(1).wait_send()

    @pl.when(co == 1)
    def _():
        core_send(0).wait_send()

    for i in range(1, 4):
        core_send(i).wait_send()
    for a in range(1, 5):
        if a in X_FIRST:
            x_send(a).wait_send()
        for t in (1, 2, 3):
            y_send(a, t).wait_send()
        o_each(a, lambda d: o_send(a, d).wait_send(), None)
    g1().wait_send()
    g2().wait_send()
    for t in range(1, 8):
        g3(t).wait_send()
        ag(t).wait_send()


def place(dq, out, gwo, dq_ref, out_ref, gwo_ref, dq_v, out_v, gwo_v, sem):
    held = ((dq, dq_v, dq_ref), (out, out_v, out_ref), (gwo, gwo_v, gwo_ref))
    come = [pltpu.make_async_copy(a, b, sem.at[0, i]) for i, (a, b, _) in enumerate(held)]
    go = [pltpu.make_async_copy(b, c, sem.at[1, i]) for i, (_, b, c) in enumerate(held)]
    for c in come:
        c.start()
    for i in range(3):
        come[i].wait()
        go[i].start()
    for c in go:
        c.wait()


def local(kv_latent, queries, grad_out, kv_up_weight, doc_ids):
    vm = pl.BlockSpec(memory_space=pltpu.VMEM)
    hbm = pl.BlockSpec(memory_space=pl.ANY)
    dma = pltpu.SemaphoreType.DMA
    V = pltpu.VMEM
    dq, out, gwo = pl.pallas_call(
        body,
        out_shape=(
            jax.ShapeDtypeStruct((ROWS, HEADS * (NOPE + ROPE)), BF16),
            jax.ShapeDtypeStruct((2, 2, 144, ROWS), BF16),
            jax.ShapeDtypeStruct((16, 512), F32),
        ),
        in_specs=[hbm] * 5,
        out_specs=(vm, vm, vm),
        scratch_shapes=[
            V((4, KEY_ROWS, ROWS), BF16), V((304, 128), BF16), V((2, 144, ROWS), BF16),
            V((ROWS, 384), BF16), V((ROWS, 256), BF16), V((512, 512), BF16), V((8, 128), jnp.int32),
            V((2, ROWS, NOPE + ROPE + MARKS), BF16), V((2, 192, ROWS), BF16), V((2, 128, ROWS), BF16), V((512, 512), BF16),
            V((4, 2, ROWS, 192), BF16), V((4, 2, ROWS, ROWS), F32), V((4, 2, ROWS, ROWS), F32),
            V((2, ROWS, 1), F32), V((2, ROWS, 1), F32), V((2, ROWS, 1), F32), V((4, 2, ROWS, 1), F32),
            V((2, ROWS, 192), F32), V((16, 2, 16, 512), F32),
            V((5, 2, 2, 144, 512), BF16), V((5, 2, 144, 512), BF16), V((5, 2, 144, 512), BF16),
            V((5, 3, 2, 144, 128), BF16), V((5, 144, 512), BF16), V((5, 144, 512), BF16), V((5, 3, 144, 128), BF16),
            V((5, 2, 144, 128), BF16), V((4, 2, 144, 128), BF16), V((2, 144, 128), BF16),
            V((16, 16, 512), F32), V((8, 2, 16, 512), BF16), V((8, 16, 512), BF16), V((8, 16, 512), BF16),
            V((7, 16, 512), BF16),
            dma((5,)), dma((4,)), dma((8,)), dma((8,)), dma((2,)), dma((4,)), dma((5,)), dma((5, 3)), dma((5, 2)), dma((7,)),
            dma((9,)),
            dma((3,)), dma((1,)), pltpu.SemaphoreType.REGULAR((3,)), dma((8,)), dma((2,)), dma((1,)), dma((5,)), dma((5,)), dma((5, 3)), dma((5, 2)), dma((7,)),
            dma((9,)),
        ],
        compiler_params=pltpu.CompilerParams(
            collective_id=0, has_side_effects=True, vmem_limit_bytes=58 * 1024 * 1024
        ),
        cost_estimate=pl.CostEstimate(flops=7_000_000_000, bytes_accessed=4_000_000, transcendentals=2_100_000),
    )(kv_latent.T, queries, grad_out, kv_up_weight, doc_ids.reshape(128, 128))
    dq, out, gwo = pl.pallas_call(
        place,
        out_shape=(
            jax.ShapeDtypeStruct((ROWS, HEADS * (NOPE + ROPE)), BF16),
            jax.ShapeDtypeStruct((WIDE, ROWS), BF16),
            jax.ShapeDtypeStruct((16, 512), F32),
        ),
        in_specs=[hbm] * 3,
        out_specs=(hbm, hbm, hbm),
        scratch_shapes=[V((ROWS, 384), BF16), V((WIDE, ROWS), BF16), V((16, 512), F32), dma((2, 3))],
    )(dq, out.reshape(WIDE, ROWS), gwo)
    return dq, out.T, gwo


def solution(mesh):
    return jax.shard_map(
        local,
        mesh=mesh,
        in_specs=(P("ctx", None), P("ctx", "head"), P("ctx", "head"), P(None, "head"), P()),
        out_specs=(P("ctx", "head"), P("ctx", None), P("ctx", "head")),
        check_vma=False,
    )
```

```python
import math

import jax
import jax.numpy as jnp
from jax import lax
from jax.experimental import pallas as pl
from jax.experimental.pallas import tpu as pltpu
from jax.sharding import PartitionSpec as P

NOPE, ROPE, VDIM, LATENT = 128, 64, 128, 512
ROWS = 512
HEADS = 2
BIG = 1e30
MESH = pl.DeviceIdType.MESH
SCALE = 1.0 / math.sqrt(NOPE + ROPE)
WIDE = LATENT + ROPE
MARKS = 32
KEY_ROWS = WIDE + MARKS
FIRST_PART = (0, 0, 0, 2, 2)
F32, BF16 = jnp.float32, jnp.bfloat16


def mm(a, b):
    return jnp.dot(a, b, preferred_element_type=F32)


def body(
    lat_hbm, q_hbm, do_hbm, w_hbm, docs_hbm, dq_hbm, out_ref, gwo_hbm,
    dq_ref, gwo_ref, s_out, kbuf, relay_buf, zrecv, q, do, w, docs, qcat, q_t, do_t, w_t, kc, e_buf, g_buf, m_ref, l_ref, x_ref, mref,
    dq_acc, gw, sbuf, crecv, ysum, yrecv, tbuf, orecv, fin, g1recv, g2buf, g2recv, g3buf, g3recv,
    s_in, s_p1, s_rel, s_fwd, s_z, s_core, s_y, s_o, s_ag, s_g,
    r_slot, r_rel, told, r_piece, r_half, r_z, r_core, r_y, r_o, r_ag, r_g,
):
    ctx = lax.axis_index("ctx")
    head = lax.axis_index("head")
    z, xl, co = ctx // 4, (ctx // 2) % 2, ctx % 2
    xh, y = head // 4, head % 4
    chip = ctx // 2

    def dev(z_, xl_, co_, xh_, y_):
        return (z_ * 4 + xl_ * 2 + co_, xh_ * 4 + y_)

    def copy(src, dst, ss, rs, to):
        return pltpu.make_async_remote_copy(
            src_ref=src, dst_ref=dst, send_sem=ss, recv_sem=rs, device_id=to, device_id_type=MESH
        )

    def lanes(k):
        return pl.ds(pl.multiple_of(k * 128, 128), 128)

    inputs = [
        pltpu.make_async_copy(docs_hbm.at[pl.ds(pl.multiple_of(chip * 8, 8), 8)], docs, s_in.at[0]),
        pltpu.make_async_copy(lat_hbm, kbuf.at[3, pl.ds(0, WIDE)], s_in.at[1]),
        pltpu.make_async_copy(w_hbm, w, s_in.at[2]),
        pltpu.make_async_copy(q_hbm, q, s_in.at[3]),
        pltpu.make_async_copy(do_hbm, do, s_in.at[4]),
    ]
    for c in inputs[:2]:
        c.start()

    barrier = pltpu.get_barrier_semaphore()
    partners = [(ctx, (head + t) % 8) for t in range(1, 8)]
    partners += [dev(z, 1 - xl, co, u // 4, u % 4) for u in range(8)]
    partners += [dev(z, xl, 1 - co, u, y) for u in range(2)]
    partners += [dev(z, 1 - xl, 1 - co, u, y) for u in range(2)]
    below, above = z > 0, z < 7
    beside = jnp.where(xl == 0, below, above)

    def greet(to):
        pl.semaphore_signal(barrier, inc=1, device_id=to, device_id_type=MESH)

    for to in partners:
        greet(to)

    @pl.when(below)
    def _():
        for k in range(2):
            greet(dev(z - 1, xl, k, xh, y))

    @pl.when(above)
    def _():
        for k in range(2):
            greet(dev(z + 1, xl, k, xh, y))

    @pl.when(beside)
    def _():
        for k in range(2):
            for u in range(2):
                greet(dev(z - 1 + 2 * xl, 1 - xl, k, u, y))

    greetings = (
        len(partners) + jnp.where(below, 2, 0) + jnp.where(above, 2, 0) + jnp.where(beside, 4, 0)
    )

    for c in inputs[2:]:
        c.start()

    inputs[0].wait()
    mine = jnp.where(co == 0, docs[0:4, :], docs[4:8, :])
    mine = jnp.concatenate([mine[i : i + 1, :] for i in range(4)], axis=1)
    marks = (lax.broadcasted_iota(jnp.int32, (MARKS, ROWS), 0) == mine).astype(F32)
    kbuf[3, WIDE:, :] = marks.astype(BF16)
    inputs[1].wait()
    pl.semaphore_wait(barrier, greetings)

    def tell(k):
        @pl.when(z >= 2**k)
        def _():
            pl.semaphore_signal(told.at[k], inc=1, device_id=dev(z - 2**k, xl, co, xh, y), device_id_type=MESH)

        @pl.when(z + 2**k < 8)
        def _():
            pl.semaphore_signal(told.at[k], inc=1, device_id=dev(z + 2**k, xl, co, xh, y), device_id_type=MESH)

    def hear(k):
        pl.semaphore_wait(told.at[k], jnp.where(z >= 2**k, 1, 0) + jnp.where(z + 2**k < 8, 1, 0))

    own = kbuf.at[3]
    sibling = dev(z, xl, 1 - co, xh, y)
    first = jnp.where(co == 1, 2, 0)
    direct = jnp.where(xl == 0, jnp.where(co == 0, 2, 0), 1)
    third = 3 - first - direct

    def full():
        slot = jnp.where(co == 0, 2, 0)
        return copy(own, kbuf.at[slot], s_p1.at[0], r_slot.at[slot], dev((z + co) % 8, xl, 1 - co, xh, y))

    def cut(ref, u):
        rows = pl.ds(pl.multiple_of((u // 4) * 304, 16), 304)
        return ref.at[rows, lanes(u % 4)]

    def piece():
        return copy(cut(own, head), relay_buf, s_p1.at[1], r_rel.at[0], dev((z + 1) % 8, 1, 1 - co, xh, y))

    def half(d):
        cols = pl.ds(d * 256, 256)
        return copy(
            own.at[:, cols], kbuf.at[1, :, cols], s_p1.at[2 + d], r_half.at[d], dev(z, 1, co, (xh + d) % 2, y)
        )

    def relay(t):
        slot = jnp.where(co == 0, 2, 0)
        return copy(
            relay_buf, cut(kbuf.at[slot], head), s_rel.at[t], r_piece.at[t], (z * 4 + co, (head + t) % 8)
        )

    def got_piece(t):
        part = cut(kbuf.at[direct], (head + 8 - t) % 8)
        return copy(part, part, s_rel.at[t], r_piece.at[t], sibling)

    def pass_piece(t):
        u = (head + 8 - t) % 8
        return copy(cut(kbuf.at[direct], u), cut(kbuf.at[1], u), s_fwd.at[t], r_slot.at[1], sibling)

    def pass_half(d):
        cols = pl.ds(d * 256, 256)
        slot = jnp.where(co == 0, 0, 2)
        return copy(kbuf.at[1, :, cols], kbuf.at[slot, :, cols], s_fwd.at[d], r_slot.at[slot], sibling)

    late = (xl == 1) & (co == 1)
    sends_full = (co == 0) | above

    @pl.when((xl == 1) & above)
    def _():
        piece().start()

    @pl.when(jnp.logical_not(late) & sends_full)
    def _():
        full().start()

    @pl.when(xl == 0)
    def _():
        half(0).start()
        half(1).start()

    def wait_slot(s):
        copy(own, kbuf.at[s], s_p1.at[0], r_slot.at[s], sibling).wait_recv()

    tell(0)

    for s in range(3):
        @pl.when((z == 0) & (s < 3 - 2 * xl - co))
        def _():
            kbuf[s, :WIDE, :] = jnp.zeros((WIDE, ROWS), BF16)
            kbuf[s, WIDE:, :] = jnp.ones((MARKS, ROWS), BF16)

    @pl.when(z == 7)
    def _():
        zrecv[...] = jnp.zeros((2, 144, ROWS), BF16)

    @pl.when(chip == 15)
    def _():
        orecv[0:2] = jnp.zeros((2, 2, 144, 128), BF16)

    for c in inputs[2:]:
        c.wait()
    w_t[...] = w[...].T
    query_mask = ((marks.T - 1.0) * BIG).astype(BF16)
    for h in range(HEADS):
        qh = q[:, h * (NOPE + ROPE) : (h + 1) * (NOPE + ROPE)]
        qcat[h] = jnp.concatenate([qh, query_mask], axis=1)
        q_t[h] = qh.T
        do_t[h] = do[:, h * VDIM : (h + 1) * VDIM].T

    @pl.when(late & above)
    def _():
        piece().wait_send()
        full().start()

    def stream(s, diagonal):
        tail = kbuf[s, LATENT:, :]
        kv = mm(w_t[...], kbuf[s, :LATENT, :]).astype(BF16)
        for h in range(HEADS):
            base = h * (NOPE + VDIM)
            keys = jnp.concatenate([kv[base : base + NOPE], tail], axis=0)
            kc[s, h] = keys[: NOPE + ROPE].T
            scores = mm(qcat[h], keys) * (SCALE * math.log2(math.e))
            if diagonal:
                query = lax.broadcasted_iota(jnp.int32, (ROWS, ROWS), 0)
                key = lax.broadcasted_iota(jnp.int32, (ROWS, ROWS), 1)
                scores = jnp.where(key <= query, scores, -BIG)
            top = jnp.max(scores, axis=1, keepdims=True)
            if not diagonal:
                top = jnp.maximum(top, m_ref[h])
            e = jnp.exp2(scores - top)
            g = mm(do[:, h * VDIM : (h + 1) * VDIM], kv[base + NOPE : base + NOPE + VDIM])
            mass = jnp.sum(e, axis=1, keepdims=True)
            cross = jnp.sum(e * g, axis=1, keepdims=True)
            if not diagonal:
                factor = jnp.exp2(m_ref[h] - top)
                mass = mass + l_ref[h] * factor
                cross = cross + x_ref[h] * factor
            m_ref[h] = top
            l_ref[h] = mass
            x_ref[h] = cross
            mref[s, h] = top
            e_buf[s, h] = e
            g_buf[s, h] = g

    @pl.when((xl == 1) & below)
    def _():
        piece().wait_recv()
        for t in (2, 6, 1, 3, 5, 7, 4, 0):
            relay(t).start()

    stream(3, True)
    hear(0)
    tell(1)
    pl.when((co == 1) | below)(lambda: wait_slot(first))
    stream(first, False)

    @pl.when((xl == 0) & below)
    def _():
        for t in (0, 4, 1, 3, 5, 7, 2, 6):
            got_piece(t).wait_recv()
            pass_piece(t).start()

    @pl.when(xl == 1)
    def _():
        for d in range(2):
            half(d).wait_recv()
            pass_half(d).start()

    stream(direct, False)
    pl.when((xl == 1) | below)(lambda: wait_slot(third))
    stream(third, False)

    @pl.when(co == 0)
    def _():
        sbuf[4, 0] = jnp.zeros((2, 144, 512), BF16)

    @pl.when(co == 1)
    def _():
        crecv[4] = jnp.zeros((2, 144, 512), BF16)

    def second(i, send, meanwhile=None):
        s = jnp.where(co == 0, (0, 1, 3, 2)[i], (3, 0, 2, 1)[i])
        grad_rope = None
        parts = []
        for h in range(HEADS):
            inverse = 1.0 / l_ref[h]
            delta = x_ref[h] * inverse
            p = e_buf[s, h] * (jnp.exp2(mref[s, h] - m_ref[h]) * inverse)
            ds = (p * (g_buf[s, h] - delta)).astype(BF16)
            pb = p.astype(BF16)
            grad_q = mm(ds, kc[s, h])
            if i == 0:
                dq_acc[h] = grad_q
            else:
                dq_acc[h] += grad_q
            grad_k = mm(q_t[h], ds) * SCALE
            grad_v = mm(do_t[h], pb)
            parts += [grad_k[:NOPE], grad_v]
            rope = grad_k[NOPE:]
            grad_rope = rope if grad_rope is None else grad_rope + rope
        dkv = jnp.concatenate(parts, axis=0).astype(BF16)
        if meanwhile is not None:
            meanwhile()
        grad = jnp.concatenate([mm(w[...], dkv), grad_rope], axis=0)
        sbuf[s + co] = grad.astype(BF16).reshape(2, 2, 144, 512)
        part = lax.dot_general(
            kbuf[s, :LATENT, :], dkv, (((1,), (1,)), ((), ())), preferred_element_type=F32
        ).reshape(16, 2, 16, 512)
        if i == 0:
            gw[...] = part
        else:
            gw[...] += part
        send()

    def core_send(i):
        a = jnp.where(co == 0, (0, 1, 3, 2)[i], (4, 1, 3, 2)[i])
        return copy(sbuf.at[a, 1 - co], crecv.at[a], s_core.at[i], r_core.at[a], sibling)

    def z_send(c):
        return copy(sbuf.at[0, c], zrecv, s_z.at[c], r_z.at[0], dev((z + 7) % 8, xl, c, xh, y))

    def y_send(a, t):
        to = (y + t) % 4
        return copy(ysum.at[a, :, :, lanes(to)], yrecv.at[a, t - 1], s_y.at[a, t - 1], r_y.at[a, t - 1], dev(z, xl, co, xh, to))

    def finish(a):
        def wait():
            copy(sbuf.at[a, 0], crecv.at[a], s_core.at[0], r_core.at[a], sibling).wait_recv()

        total = sbuf[a, co].astype(F32)
        if a == 4:
            pl.when(co == 0)(wait)
            pl.when(above)(lambda: z_send(0).wait_recv())
            total = total + zrecv[...].astype(F32)
        else:
            wait()
        ysum[a] = (total + crecv[a].astype(F32)).astype(BF16)
        for t in (2, 1, 3):
            y_send(a, t).start()

    def o_send(a, d):
        owner = (2 * chip + 29 + a) % 32
        to = (xh + d) % 2
        k = FIRST_PART[a] + d
        return copy(tbuf.at[a, to], orecv.at[k, co], s_o.at[a, d], r_o.at[k, co], (owner, to * 4 + y))

    def o_each(a, remote, here):
        def both():
            remote(0)
            remote(1)

        if a < 3:
            pl.when(chip > 0)(both)
        else:
            pl.when(co != a - 3)(lambda: remote(0))
            if here is not None:
                pl.when(co == a - 3)(here)
            remote(1)

    def stage(a):
        for t in (1, 2, 3):
            y_send(a, t).wait_recv()
        total = ysum[a, :, :, lanes(y)].astype(F32)
        for t in range(3):
            total = total + yrecv[a, t].astype(F32)
        tbuf[a] = total.astype(BF16)

        def here():
            orecv[FIRST_PART[a], co] = tbuf[a, xh]

        o_each(a, lambda d: o_send(a, d).start(), here)

    def g1():
        return copy(gw.at[:, 1 - co], g1recv, s_g.at[0], r_g.at[0], sibling)

    def g2():
        return copy(g2buf.at[:, 1 - xl], g2recv, s_g.at[1], r_g.at[1], dev(z, 1 - xl, co, xh, y))

    def g3(t):
        to = (z + t) % 8
        return copy(g3buf.at[to], g3recv.at[t - 1], s_g.at[1 + t], r_g.at[1 + t], dev(to, xl, co, xh, y))

    def arrived(k, c):
        copy(tbuf.at[0, 0], orecv.at[k, c], s_o.at[0, 0], r_o.at[k, c], sibling).wait_recv()

    def ag(t):
        return copy(
            fin, out_ref.at[:, xh, :, lanes(y)], s_ag.at[t - 1], r_ag.at[t - 1], (ctx, (head + t) % 8)
        )

    def mine_out():
        return pltpu.make_async_copy(fin, out_ref.at[:, xh, :, lanes(y)], s_out.at[2])

    def final(count, parts):
        @pl.when(chip < 15)
        def _():
            for k, c in parts[0]:
                arrived(k, c)

        for k, c in parts[1]:
            arrived(k, c)
        total = orecv[0].astype(F32)
        for k in range(1, count):
            total = total + orecv[k].astype(F32)
        fin[...] = total.astype(BF16)
        for t in (2, 6, 1, 7, 3, 5, 4):
            ag(t).start()
        mine_out().start()

    def send_first():
        @pl.when((co == 0) & below)
        def _():
            z_send(0).start()
            z_send(1).start()

        @pl.when(co == 1)
        def _():
            core_send(0).start()

    second(0, send_first)
    hear(1)
    tell(2)
    second(1, lambda: core_send(1).start())
    second(2, lambda: core_send(2).start(), lambda: finish(1))
    second(3, lambda: core_send(3).start(), lambda: finish(3))
    g1().start()
    finish(2)
    g1().wait_recv()
    g2buf[...] = (gw[:, co] + g1recv[...]).astype(BF16).reshape(8, 2, 16, 512)
    g2().start()
    stage(1)
    finish(4)
    stage(3)
    g2().wait_recv()
    g3buf[...] = (g2buf[:, xl].astype(F32) + g2recv[...].astype(F32)).astype(BF16)
    hear(2)
    for t in range(1, 8):
        g3(t).start()

    stage(4)
    stage(2)

    @pl.when(co == 0)
    def _():
        final(4, ([(0, 0), (0, 1), (1, 0), (1, 1)], [(2, 1), (3, 0), (3, 1)]))

    @pl.when(co == 1)
    def _():
        final(4, ([(0, 0), (0, 1), (1, 0), (1, 1)], [(2, 0), (3, 0), (3, 1)]))

    for h in range(HEADS):
        dq_ref[:, h * 192 : (h + 1) * 192] = (dq_acc[h] * SCALE).astype(BF16)
    dq_out = pltpu.make_async_copy(dq_ref, dq_hbm, s_out.at[0])
    dq_out.start()
    for t in range(1, 8):
        g3(t).wait_recv()
    total = g3buf[z].astype(F32)
    for t in range(7):
        total = total + g3recv[t].astype(F32)
    gwo_ref[...] = total
    gw_out = pltpu.make_async_copy(gwo_ref, gwo_hbm, s_out.at[1])
    gw_out.start()
    for t in range(1, 8):
        ag(t).wait_recv()

    mine_out().wait()
    dq_out.wait()
    gw_out.wait()
    pl.when(sends_full)(lambda: full().wait_send())
    pl.when((xl == 1) & (co == 0) & above)(lambda: piece().wait_send())

    @pl.when((xl == 1) & below)
    def _():
        for t in range(8):
            relay(t).wait_send()

    @pl.when(xl == 1)
    def _():
        for d in range(2):
            pass_half(d).wait_send()

    @pl.when(xl == 0)
    def _():
        half(0).wait_send()
        half(1).wait_send()

    @pl.when((xl == 0) & below)
    def _():
        for t in range(8):
            pass_piece(t).wait_send()

    @pl.when((co == 0) & below)
    def _():
        z_send(0).wait_send()
        z_send(1).wait_send()

    @pl.when(co == 1)
    def _():
        core_send(0).wait_send()

    for i in range(1, 4):
        core_send(i).wait_send()
    for a in range(1, 5):
        for t in (1, 2, 3):
            y_send(a, t).wait_send()
        o_each(a, lambda d: o_send(a, d).wait_send(), None)
    g1().wait_send()
    g2().wait_send()
    for t in range(1, 8):
        g3(t).wait_send()
        ag(t).wait_send()


def place(dq, out, gwo, dq_ref, out_ref, gwo_ref, dq_v, out_v, gwo_v, sem):
    held = ((dq, dq_v, dq_ref), (out, out_v, out_ref), (gwo, gwo_v, gwo_ref))
    come = [pltpu.make_async_copy(a, b, sem.at[0, i]) for i, (a, b, _) in enumerate(held)]
    go = [pltpu.make_async_copy(b, c, sem.at[1, i]) for i, (_, b, c) in enumerate(held)]
    for c in come:
        c.start()
    for i in range(3):
        come[i].wait()
        go[i].start()
    for c in go:
        c.wait()


def local(kv_latent, queries, grad_out, kv_up_weight, doc_ids):
    vm = pl.BlockSpec(memory_space=pltpu.VMEM)
    hbm = pl.BlockSpec(memory_space=pl.ANY)
    dma = pltpu.SemaphoreType.DMA
    V = pltpu.VMEM
    dq, out, gwo = pl.pallas_call(
        body,
        out_shape=(
            jax.ShapeDtypeStruct((ROWS, HEADS * (NOPE + ROPE)), BF16),
            jax.ShapeDtypeStruct((2, 2, 144, ROWS), BF16),
            jax.ShapeDtypeStruct((16, 512), F32),
        ),
        in_specs=[hbm] * 5,
        out_specs=(hbm, hbm, hbm),
        scratch_shapes=[
            V((ROWS, 384), BF16), V((16, 512), F32), dma((3,)),
            V((4, KEY_ROWS, ROWS), BF16), V((304, 128), BF16), V((2, 144, ROWS), BF16),
            V((ROWS, 384), BF16), V((ROWS, 256), BF16), V((512, 512), BF16), V((8, 128), jnp.int32),
            V((2, ROWS, NOPE + ROPE + MARKS), BF16), V((2, 192, ROWS), BF16), V((2, 128, ROWS), BF16), V((512, 512), BF16),
            V((4, 2, ROWS, 192), BF16), V((4, 2, ROWS, ROWS), F32), V((4, 2, ROWS, ROWS), F32),
            V((2, ROWS, 1), F32), V((2, ROWS, 1), F32), V((2, ROWS, 1), F32), V((4, 2, ROWS, 1), F32),
            V((2, ROWS, 192), F32), V((16, 2, 16, 512), F32),
            V((5, 2, 2, 144, 512), BF16), V((5, 2, 144, 512), BF16), V((5, 2, 144, 512), BF16),
            V((5, 3, 2, 144, 128), BF16),
            V((5, 2, 144, 128), BF16), V((4, 2, 144, 128), BF16), V((2, 144, 128), BF16),
            V((16, 16, 512), F32), V((8, 2, 16, 512), BF16), V((8, 16, 512), BF16), V((8, 16, 512), BF16),
            V((7, 16, 512), BF16),
            dma((5,)), dma((4,)), dma((8,)), dma((8,)), dma((2,)), dma((4,)), dma((5, 3)), dma((5, 2)), dma((7,)),
            dma((9,)),
            dma((3,)), dma((1,)), pltpu.SemaphoreType.REGULAR((3,)), dma((8,)), dma((2,)), dma((1,)),
            dma((5,)), dma((5, 3)), dma((5, 2)), dma((7,)), dma((9,)),
        ],
        compiler_params=pltpu.CompilerParams(
            collective_id=0, has_side_effects=True, vmem_limit_bytes=58 * 1024 * 1024
        ),
        cost_estimate=pl.CostEstimate(flops=7_000_000_000, bytes_accessed=4_000_000, transcendentals=2_100_000),
    )(kv_latent.T, queries, grad_out, kv_up_weight, doc_ids.reshape(128, 128))
    dq, out, gwo = pl.pallas_call(
        place,
        out_shape=(
            jax.ShapeDtypeStruct((ROWS, HEADS * (NOPE + ROPE)), BF16),
            jax.ShapeDtypeStruct((WIDE, ROWS), BF16),
            jax.ShapeDtypeStruct((16, 512), F32),
        ),
        in_specs=[hbm] * 3,
        out_specs=(hbm, hbm, hbm),
        scratch_shapes=[V((ROWS, 384), BF16), V((WIDE, ROWS), BF16), V((16, 512), F32), dma((2, 3))],
    )(dq, out.reshape(WIDE, ROWS), gwo)
    return dq, out.T, gwo


def solution(mesh):
    return jax.shard_map(
        local,
        mesh=mesh,
        in_specs=(P("ctx", None), P("ctx", "head"), P("ctx", "head"), P(None, "head"), P()),
        out_specs=(P("ctx", "head"), P("ctx", None), P("ctx", "head")),
        check_vma=False,
    )
```

```python
import math

import jax
import jax.numpy as jnp
from jax import lax
from jax.experimental import pallas as pl
from jax.experimental.pallas import tpu as pltpu
from jax.sharding import PartitionSpec as P

NOPE, ROPE, VDIM, LATENT = 128, 64, 128, 512
ROWS = 512
HEADS = 2
BIG = 1e30
MESH = pl.DeviceIdType.MESH
SCALE = 1.0 / math.sqrt(NOPE + ROPE)
WIDE = LATENT + ROPE
MARKS = 32
KEY_ROWS = WIDE + MARKS
FIRST_PART = (0, 0, 0, 2, 2)
F32, BF16 = jnp.float32, jnp.bfloat16


def mm(a, b):
    return jnp.dot(a, b, preferred_element_type=F32)


def body(
    lat_hbm, q_hbm, do_hbm, w_hbm, docs_hbm, dq_hbm, out_ref, gwo_hbm,
    dq_ref, gwo_ref, s_out, kbuf, relay_buf, zrecv, q, do, w, docs, qcat, q_t, do_t, w_t, kc, e_buf, g_buf, m_ref, l_ref, x_ref, mref,
    dq_acc, gw, sbuf, crecv, ysum, yrecv, tbuf, orecv, fin, g1recv, g2buf, g2recv, g3buf, g3recv,
    s_in, s_p1, s_rel, s_fwd, s_z, s_core, s_y, s_o, s_ag, s_g,
    r_slot, r_rel, told, r_piece, r_half, r_z, r_core, r_y, r_o, r_ag, r_g,
):
    ctx = lax.axis_index("ctx")
    head = lax.axis_index("head")
    z, xl, co = ctx // 4, (ctx // 2) % 2, ctx % 2
    xh, y = head // 4, head % 4
    chip = ctx // 2

    def dev(z_, xl_, co_, xh_, y_):
        return (z_ * 4 + xl_ * 2 + co_, xh_ * 4 + y_)

    def copy(src, dst, ss, rs, to):
        return pltpu.make_async_remote_copy(
            src_ref=src, dst_ref=dst, send_sem=ss, recv_sem=rs, device_id=to, device_id_type=MESH
        )

    def lanes(k):
        return pl.ds(pl.multiple_of(k * 128, 128), 128)

    inputs = [
        pltpu.make_async_copy(docs_hbm.at[pl.ds(pl.multiple_of(chip * 8, 8), 8)], docs, s_in.at[0]),
        pltpu.make_async_copy(lat_hbm, kbuf.at[3, pl.ds(0, WIDE)], s_in.at[1]),
        pltpu.make_async_copy(w_hbm, w, s_in.at[2]),
        pltpu.make_async_copy(q_hbm, q, s_in.at[3]),
        pltpu.make_async_copy(do_hbm, do, s_in.at[4]),
    ]
    for c in inputs[:2]:
        c.start()

    barrier = pltpu.get_barrier_semaphore()
    partners = [(ctx, (head + t) % 8) for t in range(1, 8)]
    partners += [dev(z, 1 - xl, co, u // 4, u % 4) for u in range(8)]
    partners += [dev(z, xl, 1 - co, u, y) for u in range(2)]
    partners += [dev(z, 1 - xl, 1 - co, u, y) for u in range(2)]
    below, above = z > 0, z < 7
    beside = jnp.where(xl == 0, below, above)

    def greet(to):
        pl.semaphore_signal(barrier, inc=1, device_id=to, device_id_type=MESH)

    for to in partners:
        greet(to)

    @pl.when(below)
    def _():
        for k in range(2):
            greet(dev(z - 1, xl, k, xh, y))

    @pl.when(above)
    def _():
        for k in range(2):
            greet(dev(z + 1, xl, k, xh, y))

    @pl.when(beside)
    def _():
        for k in range(2):
            for u in range(2):
                greet(dev(z - 1 + 2 * xl, 1 - xl, k, u, y))

    greetings = (
        len(partners) + jnp.where(below, 2, 0) + jnp.where(above, 2, 0) + jnp.where(beside, 4, 0)
    )

    for c in inputs[2:]:
        c.start()

    inputs[0].wait()
    mine = jnp.where(co == 0, docs[0:4, :], docs[4:8, :])
    mine = jnp.concatenate([mine[i : i + 1, :] for i in range(4)], axis=1)
    marks = (lax.broadcasted_iota(jnp.int32, (MARKS, ROWS), 0) == mine).astype(F32)
    kbuf[3, WIDE:, :] = marks.astype(BF16)
    inputs[1].wait()
    pl.semaphore_wait(barrier, greetings)

    def tell(k):
        @pl.when(z >= 2**k)
        def _():
            pl.semaphore_signal(told.at[k], inc=1, device_id=dev(z - 2**k, xl, co, xh, y), device_id_type=MESH)

        @pl.when(z + 2**k < 8)
        def _():
            pl.semaphore_signal(told.at[k], inc=1, device_id=dev(z + 2**k, xl, co, xh, y), device_id_type=MESH)

    def hear(k):
        pl.semaphore_wait(told.at[k], jnp.where(z >= 2**k, 1, 0) + jnp.where(z + 2**k < 8, 1, 0))

    own = kbuf.at[3]
    sibling = dev(z, xl, 1 - co, xh, y)
    first = jnp.where(co == 1, 2, 0)
    direct = jnp.where(xl == 0, jnp.where(co == 0, 2, 0), 1)
    third = 3 - first - direct

    def full():
        slot = jnp.where(co == 0, 2, 0)
        return copy(own, kbuf.at[slot], s_p1.at[0], r_slot.at[slot], dev((z + co) % 8, xl, 1 - co, xh, y))

    def cut(ref, u):
        rows = pl.ds(pl.multiple_of((u // 4) * 304, 16), 304)
        return ref.at[rows, lanes(u % 4)]

    def piece():
        return copy(cut(own, head), relay_buf, s_p1.at[1], r_rel.at[0], dev((z + 1) % 8, 1, 1 - co, xh, y))

    def half(d):
        cols = pl.ds(d * 256, 256)
        return copy(
            own.at[:, cols], kbuf.at[1, :, cols], s_p1.at[2 + d], r_half.at[d], dev(z, 1, co, (xh + d) % 2, y)
        )

    def relay(t):
        slot = jnp.where(co == 0, 2, 0)
        return copy(
            relay_buf, cut(kbuf.at[slot], head), s_rel.at[t], r_piece.at[t], (z * 4 + co, (head + t) % 8)
        )

    def got_piece(t):
        part = cut(kbuf.at[direct], (head + 8 - t) % 8)
        return copy(part, part, s_rel.at[t], r_piece.at[t], sibling)

    def pass_piece(t):
        u = (head + 8 - t) % 8
        return copy(cut(kbuf.at[direct], u), cut(kbuf.at[1], u), s_fwd.at[t], r_slot.at[1], sibling)

    def pass_half(d):
        cols = pl.ds(d * 256, 256)
        slot = jnp.where(co == 0, 0, 2)
        return copy(kbuf.at[1, :, cols], kbuf.at[slot, :, cols], s_fwd.at[d], r_slot.at[slot], sibling)

    late = (xl == 1) & (co == 1)
    sends_full = (co == 0) | above

    @pl.when((xl == 1) & above)
    def _():
        piece().start()

    @pl.when(jnp.logical_not(late) & sends_full)
    def _():
        full().start()

    @pl.when(xl == 0)
    def _():
        half(0).start()
        half(1).start()

    def wait_slot(s):
        copy(own, kbuf.at[s], s_p1.at[0], r_slot.at[s], sibling).wait_recv()

    tell(0)

    for s in range(3):
        @pl.when((z == 0) & (s < 3 - 2 * xl - co))
        def _():
            kbuf[s, :WIDE, :] = jnp.zeros((WIDE, ROWS), BF16)
            kbuf[s, WIDE:, :] = jnp.ones((MARKS, ROWS), BF16)

    @pl.when(z == 7)
    def _():
        zrecv[...] = jnp.zeros((2, 144, ROWS), BF16)

    @pl.when(chip == 15)
    def _():
        orecv[0:2] = jnp.zeros((2, 2, 144, 128), BF16)

    for c in inputs[2:]:
        c.wait()
    w_t[...] = w[...].T
    query_mask = ((marks.T - 1.0) * BIG).astype(BF16)
    for h in range(HEADS):
        qh = q[:, h * (NOPE + ROPE) : (h + 1) * (NOPE + ROPE)]
        qcat[h] = jnp.concatenate([qh, query_mask], axis=1)
        q_t[h] = qh.T
        do_t[h] = do[:, h * VDIM : (h + 1) * VDIM].T

    @pl.when(late & above)
    def _():
        piece().wait_send()
        full().start()

    def stream(s, diagonal):
        tail = kbuf[s, LATENT:, :]
        kv = mm(w_t[...], kbuf[s, :LATENT, :]).astype(BF16)
        for h in range(HEADS):
            base = h * (NOPE + VDIM)
            keys = jnp.concatenate([kv[base : base + NOPE], tail], axis=0)
            kc[s, h] = keys[: NOPE + ROPE].T
            scores = mm(qcat[h], keys) * (SCALE * math.log2(math.e))
            if diagonal:
                query = lax.broadcasted_iota(jnp.int32, (ROWS, ROWS), 0)
                key = lax.broadcasted_iota(jnp.int32, (ROWS, ROWS), 1)
                scores = jnp.where(key <= query, scores, -BIG)
            top = jnp.max(scores, axis=1, keepdims=True)
            if not diagonal:
                top = jnp.maximum(top, m_ref[h])
            e = jnp.exp2(scores - top)
            g = mm(do[:, h * VDIM : (h + 1) * VDIM], kv[base + NOPE : base + NOPE + VDIM])
            mass = jnp.sum(e, axis=1, keepdims=True)
            cross = jnp.sum(e * g, axis=1, keepdims=True)
            if not diagonal:
                factor = jnp.exp2(m_ref[h] - top)
                mass = mass + l_ref[h] * factor
                cross = cross + x_ref[h] * factor
            m_ref[h] = top
            l_ref[h] = mass
            x_ref[h] = cross
            mref[s, h] = top
            e_buf[s, h] = e
            g_buf[s, h] = g

    @pl.when((xl == 1) & below)
    def _():
        piece().wait_recv()
        for t in (2, 6, 1, 3, 5, 7, 4, 0):
            relay(t).start()

    stream(3, True)
    hear(0)
    tell(1)
    pl.when((co == 1) | below)(lambda: wait_slot(first))
    stream(first, False)

    @pl.when((xl == 0) & below)
    def _():
        for t in (0, 4, 1, 3, 5, 7, 2, 6):
            got_piece(t).wait_recv()
            pass_piece(t).start()

    @pl.when(xl == 1)
    def _():
        for d in range(2):
            half(d).wait_recv()
            pass_half(d).start()

    stream(direct, False)
    pl.when((xl == 1) | below)(lambda: wait_slot(third))
    stream(third, False)

    @pl.when(co == 0)
    def _():
        sbuf[4, 0] = jnp.zeros((2, 144, 512), BF16)

    @pl.when(co == 1)
    def _():
        crecv[4] = jnp.zeros((2, 144, 512), BF16)

    def second(i, send, meanwhile=None):
        s = jnp.where(co == 0, (0, 1, 3, 2)[i], (3, 0, 2, 1)[i])
        grad_rope = None
        parts = []
        for h in range(HEADS):
            inverse = 1.0 / l_ref[h]
            delta = x_ref[h] * inverse
            p = e_buf[s, h] * (jnp.exp2(mref[s, h] - m_ref[h]) * inverse)
            ds = (p * (g_buf[s, h] - delta)).astype(BF16)
            pb = p.astype(BF16)
            grad_q = mm(ds, kc[s, h])
            if i == 0:
                dq_acc[h] = grad_q
            else:
                dq_acc[h] += grad_q
            grad_k = mm(q_t[h], ds) * SCALE
            grad_v = mm(do_t[h], pb)
            parts += [grad_k[:NOPE], grad_v]
            rope = grad_k[NOPE:]
            grad_rope = rope if grad_rope is None else grad_rope + rope
        dkv = jnp.concatenate(parts, axis=0).astype(BF16)
        if meanwhile is not None:
            meanwhile()
        grad = jnp.concatenate([mm(w[...], dkv), grad_rope], axis=0)
        sbuf[s + co] = grad.astype(BF16).reshape(2, 2, 144, 512)
        part = lax.dot_general(
            kbuf[s, :LATENT, :], dkv, (((1,), (1,)), ((), ())), preferred_element_type=F32
        ).reshape(16, 2, 16, 512)
        if i == 0:
            gw[...] = part
        else:
            gw[...] += part
        send()

    def core_send(i):
        a = jnp.where(co == 0, (0, 1, 3, 2)[i], (4, 1, 3, 2)[i])
        return copy(sbuf.at[a, 1 - co], crecv.at[a], s_core.at[i], r_core.at[a], sibling)

    def z_send(c):
        return copy(sbuf.at[0, c], zrecv, s_z.at[c], r_z.at[0], dev((z + 7) % 8, xl, c, xh, y))

    def y_send(a, t):
        to = (y + t) % 4
        return copy(ysum.at[a, :, :, lanes(to)], yrecv.at[a, t - 1], s_y.at[a, t - 1], r_y.at[a, t - 1], dev(z, xl, co, xh, to))

    def finish(a):
        def wait():
            copy(sbuf.at[a, 0], crecv.at[a], s_core.at[0], r_core.at[a], sibling).wait_recv()

        total = sbuf[a, co].astype(F32)
        if a == 4:
            pl.when(co == 0)(wait)
            pl.when(above)(lambda: z_send(0).wait_recv())
            total = total + zrecv[...].astype(F32)
        else:
            wait()
        ysum[a] = (total + crecv[a].astype(F32)).astype(BF16)
        for t in (2, 1, 3):
            y_send(a, t).start()

    def o_send(a, d):
        owner = (2 * chip + 29 + a) % 32
        to = (xh + d) % 2
        k = FIRST_PART[a] + d
        return copy(tbuf.at[a, to], orecv.at[k, co], s_o.at[a, d], r_o.at[k, co], (owner, to * 4 + y))

    def o_each(a, remote, here):
        def both():
            remote(0)
            remote(1)

        if a < 3:
            pl.when(chip > 0)(both)
        else:
            pl.when(co != a - 3)(lambda: remote(0))
            if here is not None:
                pl.when(co == a - 3)(here)
            remote(1)

    def stage(a):
        for t in (1, 2, 3):
            y_send(a, t).wait_recv()
        total = ysum[a, :, :, lanes(y)].astype(F32)
        for t in range(3):
            total = total + yrecv[a, t].astype(F32)
        tbuf[a] = total.astype(BF16)

        def here():
            orecv[FIRST_PART[a], co] = tbuf[a, xh]

        o_each(a, lambda d: o_send(a, d).start(), here)

    def g1():
        return copy(gw.at[:, 1 - co], g1recv, s_g.at[0], r_g.at[0], sibling)

    def g2():
        return copy(g2buf.at[:, 1 - xl], g2recv, s_g.at[1], r_g.at[1], dev(z, 1 - xl, co, xh, y))

    def g3(t):
        to = (z + t) % 8
        return copy(g3buf.at[to], g3recv.at[t - 1], s_g.at[1 + t], r_g.at[1 + t], dev(to, xl, co, xh, y))

    def arrived(k, c):
        copy(tbuf.at[0, 0], orecv.at[k, c], s_o.at[0, 0], r_o.at[k, c], sibling).wait_recv()

    def ag(t):
        return copy(
            fin, out_ref.at[:, xh, :, lanes(y)], s_ag.at[t - 1], r_ag.at[t - 1], (ctx, (head + t) % 8)
        )

    def mine_out():
        return pltpu.make_async_copy(fin, out_ref.at[:, xh, :, lanes(y)], s_out.at[2])

    def final(count, parts):
        @pl.when(chip < 15)
        def _():
            for k, c in parts[0]:
                arrived(k, c)

        for k, c in parts[1]:
            arrived(k, c)
        total = orecv[0].astype(F32)
        for k in range(1, count):
            total = total + orecv[k].astype(F32)
        fin[...] = total.astype(BF16)
        for t in (2, 6, 1, 7, 3, 5, 4):
            ag(t).start()
        mine_out().start()

    def send_first():
        @pl.when((co == 0) & below)
        def _():
            z_send(0).start()
            z_send(1).start()

        @pl.when(co == 1)
        def _():
            core_send(0).start()

    second(0, send_first)
    hear(1)
    tell(2)
    second(1, lambda: core_send(1).start())
    second(2, lambda: core_send(2).start(), lambda: finish(1))
    second(3, lambda: core_send(3).start(), lambda: finish(3))
    g1().start()
    finish(2)
    g1().wait_recv()
    g2buf[...] = (gw[:, co] + g1recv[...]).astype(BF16).reshape(8, 2, 16, 512)
    g2().start()
    stage(1)
    finish(4)
    stage(3)
    g2().wait_recv()
    g3buf[...] = (g2buf[:, xl].astype(F32) + g2recv[...].astype(F32)).astype(BF16)
    hear(2)
    for t in range(1, 8):
        g3(t).start()

    stage(2)
    stage(4)

    @pl.when(co == 0)
    def _():
        final(4, ([(0, 0), (0, 1), (1, 0), (1, 1)], [(2, 1), (3, 0), (3, 1)]))

    @pl.when(co == 1)
    def _():
        final(4, ([(0, 0), (0, 1), (1, 0), (1, 1)], [(2, 0), (3, 0), (3, 1)]))

    for h in range(HEADS):
        dq_ref[:, h * 192 : (h + 1) * 192] = (dq_acc[h] * SCALE).astype(BF16)
    dq_out = pltpu.make_async_copy(dq_ref, dq_hbm, s_out.at[0])
    dq_out.start()
    for t in range(1, 8):
        g3(t).wait_recv()
    total = g3buf[z].astype(F32)
    for t in range(7):
        total = total + g3recv[t].astype(F32)
    gwo_ref[...] = total
    gw_out = pltpu.make_async_copy(gwo_ref, gwo_hbm, s_out.at[1])
    gw_out.start()
    for t in range(1, 8):
        ag(t).wait_recv()

    mine_out().wait()
    dq_out.wait()
    gw_out.wait()
    pl.when(sends_full)(lambda: full().wait_send())
    pl.when((xl == 1) & (co == 0) & above)(lambda: piece().wait_send())

    @pl.when((xl == 1) & below)
    def _():
        for t in range(8):
            relay(t).wait_send()

    @pl.when(xl == 1)
    def _():
        for d in range(2):
            pass_half(d).wait_send()

    @pl.when(xl == 0)
    def _():
        half(0).wait_send()
        half(1).wait_send()

    @pl.when((xl == 0) & below)
    def _():
        for t in range(8):
            pass_piece(t).wait_send()

    @pl.when((co == 0) & below)
    def _():
        z_send(0).wait_send()
        z_send(1).wait_send()

    @pl.when(co == 1)
    def _():
        core_send(0).wait_send()

    for i in range(1, 4):
        core_send(i).wait_send()
    for a in range(1, 5):
        for t in (1, 2, 3):
            y_send(a, t).wait_send()
        o_each(a, lambda d: o_send(a, d).wait_send(), None)
    g1().wait_send()
    g2().wait_send()
    for t in range(1, 8):
        g3(t).wait_send()
        ag(t).wait_send()


def place(dq, out, gwo, dq_ref, out_ref, gwo_ref, dq_v, out_v, gwo_v, sem):
    held = ((dq, dq_v, dq_ref), (out, out_v, out_ref), (gwo, gwo_v, gwo_ref))
    come = [pltpu.make_async_copy(a, b, sem.at[0, i]) for i, (a, b, _) in enumerate(held)]
    go = [pltpu.make_async_copy(b, c, sem.at[1, i]) for i, (_, b, c) in enumerate(held)]
    for c in come:
        c.start()
    for i in range(3):
        come[i].wait()
        go[i].start()
    for c in go:
        c.wait()


def local(kv_latent, queries, grad_out, kv_up_weight, doc_ids):
    vm = pl.BlockSpec(memory_space=pltpu.VMEM)
    hbm = pl.BlockSpec(memory_space=pl.ANY)
    dma = pltpu.SemaphoreType.DMA
    V = pltpu.VMEM
    dq, out, gwo = pl.pallas_call(
        body,
        out_shape=(
            jax.ShapeDtypeStruct((ROWS, HEADS * (NOPE + ROPE)), BF16),
            jax.ShapeDtypeStruct((2, 2, 144, ROWS), BF16),
            jax.ShapeDtypeStruct((16, 512), F32),
        ),
        in_specs=[hbm] * 5,
        out_specs=(hbm, hbm, hbm),
        scratch_shapes=[
            V((ROWS, 384), BF16), V((16, 512), F32), dma((3,)),
            V((4, KEY_ROWS, ROWS), BF16), V((304, 128), BF16), V((2, 144, ROWS), BF16),
            V((ROWS, 384), BF16), V((ROWS, 256), BF16), V((512, 512), BF16), V((8, 128), jnp.int32),
            V((2, ROWS, NOPE + ROPE + MARKS), BF16), V((2, 192, ROWS), BF16), V((2, 128, ROWS), BF16), V((512, 512), BF16),
            V((4, 2, ROWS, 192), BF16), V((4, 2, ROWS, ROWS), F32), V((4, 2, ROWS, ROWS), F32),
            V((2, ROWS, 1), F32), V((2, ROWS, 1), F32), V((2, ROWS, 1), F32), V((4, 2, ROWS, 1), F32),
            V((2, ROWS, 192), F32), V((16, 2, 16, 512), F32),
            V((5, 2, 2, 144, 512), BF16), V((5, 2, 144, 512), BF16), V((5, 2, 144, 512), BF16),
            V((5, 3, 2, 144, 128), BF16),
            V((5, 2, 144, 128), BF16), V((4, 2, 144, 128), BF16), V((2, 144, 128), BF16),
            V((16, 16, 512), F32), V((8, 2, 16, 512), BF16), V((8, 16, 512), BF16), V((8, 16, 512), BF16),
            V((7, 16, 512), BF16),
            dma((5,)), dma((4,)), dma((8,)), dma((8,)), dma((2,)), dma((4,)), dma((5, 3)), dma((5, 2)), dma((7,)),
            dma((9,)),
            dma((3,)), dma((1,)), pltpu.SemaphoreType.REGULAR((3,)), dma((8,)), dma((2,)), dma((1,)),
            dma((5,)), dma((5, 3)), dma((5, 2)), dma((7,)), dma((9,)),
        ],
        compiler_params=pltpu.CompilerParams(
            collective_id=0, has_side_effects=True, vmem_limit_bytes=58 * 1024 * 1024
        ),
        cost_estimate=pl.CostEstimate(flops=7_000_000_000, bytes_accessed=4_000_000, transcendentals=2_100_000),
    )(kv_latent.T, queries, grad_out, kv_up_weight, doc_ids.reshape(128, 128))
    dq, out, gwo = pl.pallas_call(
        place,
        out_shape=(
            jax.ShapeDtypeStruct((ROWS, HEADS * (NOPE + ROPE)), BF16),
            jax.ShapeDtypeStruct((WIDE, ROWS), BF16),
            jax.ShapeDtypeStruct((16, 512), F32),
        ),
        in_specs=[hbm] * 3,
        out_specs=(hbm, hbm, hbm),
        scratch_shapes=[V((ROWS, 384), BF16), V((WIDE, ROWS), BF16), V((16, 512), F32), dma((2, 3))],
    )(dq, out.reshape(WIDE, ROWS), gwo)
    return dq, out.T, gwo


def solution(mesh):
    return jax.shard_map(
        local,
        mesh=mesh,
        in_specs=(P("ctx", None), P("ctx", "head"), P("ctx", "head"), P(None, "head"), P()),
        out_specs=(P("ctx", "head"), P("ctx", None), P("ctx", "head")),
        check_vma=False,
    )
```

```python
import math

import jax
import jax.numpy as jnp
from jax import lax
from jax.experimental import pallas as pl
from jax.experimental.pallas import tpu as pltpu
from jax.sharding import PartitionSpec as P

NOPE, ROPE, VDIM, LATENT = 128, 64, 128, 512
ROWS = 512
HEADS = 2
BIG = 1e30
MESH = pl.DeviceIdType.MESH
SCALE = 1.0 / math.sqrt(NOPE + ROPE)
WIDE = LATENT + ROPE
MARKS = 32
KEY_ROWS = WIDE + MARKS
FIRST_PART = (0, 0, 0, 2, 2)
F32, BF16 = jnp.float32, jnp.bfloat16


def mm(a, b):
    return jnp.dot(a, b, preferred_element_type=F32)


def body(
    lat_hbm, q_hbm, do_hbm, w_hbm, docs_hbm, dq_hbm, out_ref, gwo_hbm,
    dq_ref, gwo_ref, s_out, kbuf, relay_buf, zrecv, q, do, w, docs, qcat, q_t, do_t, w_t, kc, e_buf, g_buf, m_ref, l_ref, x_ref, mref,
    dq_acc, gw, sbuf, crecv, ysum, yrecv, tbuf, orecv, fin, g1recv, g2buf, g2recv, g3buf, g3recv,
    s_in, s_p1, s_rel, s_fwd, s_z, s_core, s_y, s_o, s_ag, s_g,
    r_slot, r_rel, told, r_piece, r_half, r_z, r_core, r_y, r_o, r_ag, r_g,
):
    ctx = lax.axis_index("ctx")
    head = lax.axis_index("head")
    z, xl, co = ctx // 4, (ctx // 2) % 2, ctx % 2
    xh, y = head // 4, head % 4
    chip = ctx // 2

    def dev(z_, xl_, co_, xh_, y_):
        return (z_ * 4 + xl_ * 2 + co_, xh_ * 4 + y_)

    def copy(src, dst, ss, rs, to):
        return pltpu.make_async_remote_copy(
            src_ref=src, dst_ref=dst, send_sem=ss, recv_sem=rs, device_id=to, device_id_type=MESH
        )

    def lanes(k):
        return pl.ds(pl.multiple_of(k * 128, 128), 128)

    inputs = [
        pltpu.make_async_copy(docs_hbm.at[pl.ds(pl.multiple_of(chip * 8, 8), 8)], docs, s_in.at[0]),
        pltpu.make_async_copy(lat_hbm, kbuf.at[3, pl.ds(0, WIDE)], s_in.at[1]),
        pltpu.make_async_copy(w_hbm, w, s_in.at[2]),
        pltpu.make_async_copy(q_hbm, q, s_in.at[3]),
        pltpu.make_async_copy(do_hbm, do, s_in.at[4]),
    ]
    for c in inputs[:2]:
        c.start()

    barrier = pltpu.get_barrier_semaphore()
    partners = [(ctx, (head + t) % 8) for t in range(1, 8)]
    partners += [dev(z, 1 - xl, co, u // 4, u % 4) for u in range(8)]
    partners += [dev(z, xl, 1 - co, u, y) for u in range(2)]
    partners += [dev(z, 1 - xl, 1 - co, u, y) for u in range(2)]
    below, above = z > 0, z < 7
    beside = jnp.where(xl == 0, below, above)

    def greet(to):
        pl.semaphore_signal(barrier, inc=1, device_id=to, device_id_type=MESH)

    for to in partners:
        greet(to)

    @pl.when(below)
    def _():
        for k in range(2):
            greet(dev(z - 1, xl, k, xh, y))

    @pl.when(above)
    def _():
        for k in range(2):
            greet(dev(z + 1, xl, k, xh, y))

    @pl.when(beside)
    def _():
        for k in range(2):
            for u in range(2):
                greet(dev(z - 1 + 2 * xl, 1 - xl, k, u, y))

    greetings = (
        len(partners) + jnp.where(below, 2, 0) + jnp.where(above, 2, 0) + jnp.where(beside, 4, 0)
    )

    for c in inputs[2:]:
        c.start()

    inputs[0].wait()
    mine = jnp.where(co == 0, docs[0:4, :], docs[4:8, :])
    mine = jnp.concatenate([mine[i : i + 1, :] for i in range(4)], axis=1)
    marks = (lax.broadcasted_iota(jnp.int32, (MARKS, ROWS), 0) == mine).astype(F32)
    kbuf[3, WIDE:, :] = marks.astype(BF16)
    inputs[1].wait()
    pl.semaphore_wait(barrier, greetings)

    def tell(k):
        @pl.when(z >= 2**k)
        def _():
            pl.semaphore_signal(told.at[k], inc=1, device_id=dev(z - 2**k, xl, co, xh, y), device_id_type=MESH)

        @pl.when(z + 2**k < 8)
        def _():
            pl.semaphore_signal(told.at[k], inc=1, device_id=dev(z + 2**k, xl, co, xh, y), device_id_type=MESH)

    def hear(k):
        pl.semaphore_wait(told.at[k], jnp.where(z >= 2**k, 1, 0) + jnp.where(z + 2**k < 8, 1, 0))

    own = kbuf.at[3]
    sibling = dev(z, xl, 1 - co, xh, y)
    first = jnp.where(co == 1, 2, 0)
    direct = jnp.where(xl == 0, jnp.where(co == 0, 2, 0), 1)
    third = 3 - first - direct

    def full():
        slot = jnp.where(co == 0, 2, 0)
        return copy(own, kbuf.at[slot], s_p1.at[0], r_slot.at[slot], dev((z + co) % 8, xl, 1 - co, xh, y))

    def cut(ref, u):
        rows = pl.ds(pl.multiple_of((u // 4) * 304, 16), 304)
        return ref.at[rows, lanes(u % 4)]

    def piece():
        return copy(cut(own, head), relay_buf, s_p1.at[1], r_rel.at[0], dev((z + 1) % 8, 1, 1 - co, xh, y))

    def half(d):
        cols = pl.ds(d * 256, 256)
        return copy(
            own.at[:, cols], kbuf.at[1, :, cols], s_p1.at[2 + d], r_half.at[d], dev(z, 1, co, (xh + d) % 2, y)
        )

    def relay(t):
        slot = jnp.where(co == 0, 2, 0)
        return copy(
            relay_buf, cut(kbuf.at[slot], head), s_rel.at[t], r_piece.at[t], (z * 4 + co, (head + t) % 8)
        )

    def got_piece(t):
        part = cut(kbuf.at[direct], (head + 8 - t) % 8)
        return copy(part, part, s_rel.at[t], r_piece.at[t], sibling)

    def pass_piece(t):
        u = (head + 8 - t) % 8
        return copy(cut(kbuf.at[direct], u), cut(kbuf.at[1], u), s_fwd.at[t], r_slot.at[1], sibling)

    def pass_half(d):
        cols = pl.ds(d * 256, 256)
        slot = jnp.where(co == 0, 0, 2)
        return copy(kbuf.at[1, :, cols], kbuf.at[slot, :, cols], s_fwd.at[d], r_slot.at[slot], sibling)

    late = (xl == 1) & (co == 1)
    sends_full = (co == 0) | above

    @pl.when((xl == 1) & above)
    def _():
        piece().start()

    @pl.when(jnp.logical_not(late) & sends_full)
    def _():
        full().start()

    @pl.when(xl == 0)
    def _():
        half(0).start()
        half(1).start()

    def wait_slot(s):
        copy(own, kbuf.at[s], s_p1.at[0], r_slot.at[s], sibling).wait_recv()

    tell(0)

    for s in range(3):
        @pl.when((z == 0) & (s < 3 - 2 * xl - co))
        def _():
            kbuf[s, :WIDE, :] = jnp.zeros((WIDE, ROWS), BF16)
            kbuf[s, WIDE:, :] = jnp.ones((MARKS, ROWS), BF16)

    @pl.when(z == 7)
    def _():
        zrecv[...] = jnp.zeros((2, 144, ROWS), BF16)

    @pl.when(chip == 15)
    def _():
        orecv[0:2] = jnp.zeros((2, 2, 144, 128), BF16)

    for c in inputs[2:]:
        c.wait()
    w_t[...] = w[...].T
    query_mask = ((marks.T - 1.0) * BIG).astype(BF16)
    for h in range(HEADS):
        qh = q[:, h * (NOPE + ROPE) : (h + 1) * (NOPE + ROPE)]
        qcat[h] = jnp.concatenate([qh, query_mask], axis=1)
        q_t[h] = qh.T
        do_t[h] = do[:, h * VDIM : (h + 1) * VDIM].T

    @pl.when(late & above)
    def _():
        piece().wait_send()
        full().start()

    def stream(s, diagonal):
        tail = kbuf[s, LATENT:, :]
        kv = mm(w_t[...], kbuf[s, :LATENT, :]).astype(BF16)
        for h in range(HEADS):
            base = h * (NOPE + VDIM)
            keys = jnp.concatenate([kv[base : base + NOPE], tail], axis=0)
            kc[s, h] = keys[: NOPE + ROPE].T
            scores = mm(qcat[h], keys) * (SCALE * math.log2(math.e))
            if diagonal:
                query = lax.broadcasted_iota(jnp.int32, (ROWS, ROWS), 0)
                key = lax.broadcasted_iota(jnp.int32, (ROWS, ROWS), 1)
                scores = jnp.where(key <= query, scores, -BIG)
            top = jnp.max(scores, axis=1, keepdims=True)
            if not diagonal:
                top = jnp.maximum(top, m_ref[h])
            e = jnp.exp2(scores - top)
            g = mm(do[:, h * VDIM : (h + 1) * VDIM], kv[base + NOPE : base + NOPE + VDIM])
            mass = jnp.sum(e, axis=1, keepdims=True)
            cross = jnp.sum(e * g, axis=1, keepdims=True)
            if not diagonal:
                factor = jnp.exp2(m_ref[h] - top)
                mass = mass + l_ref[h] * factor
                cross = cross + x_ref[h] * factor
            m_ref[h] = top
            l_ref[h] = mass
            x_ref[h] = cross
            mref[s, h] = top
            e_buf[s, h] = e
            g_buf[s, h] = g

    @pl.when((xl == 1) & below)
    def _():
        piece().wait_recv()
        for t in (2, 6, 1, 3, 5, 7, 4, 0):
            relay(t).start()

    stream(3, True)
    hear(0)
    tell(1)
    pl.when((co == 1) | below)(lambda: wait_slot(first))
    stream(first, False)

    @pl.when((xl == 0) & below)
    def _():
        for t in (0, 4, 1, 3, 5, 7, 2, 6):
            got_piece(t).wait_recv()
            pass_piece(t).start()

    @pl.when(xl == 1)
    def _():
        for d in range(2):
            half(d).wait_recv()
            pass_half(d).start()

    stream(direct, False)
    pl.when((xl == 1) | below)(lambda: wait_slot(third))
    stream(third, False)

    @pl.when(co == 0)
    def _():
        sbuf[4, 0] = jnp.zeros((2, 144, 512), BF16)

    @pl.when(co == 1)
    def _():
        crecv[4] = jnp.zeros((2, 144, 512), BF16)

    def second(i, send, meanwhile=None):
        s = jnp.where(co == 0, (0, 1, 3, 2)[i], (3, 0, 2, 1)[i])
        grad_rope = None
        parts = []
        for h in range(HEADS):
            inverse = 1.0 / l_ref[h]
            delta = x_ref[h] * inverse
            p = e_buf[s, h] * (jnp.exp2(mref[s, h] - m_ref[h]) * inverse)
            ds = (p * (g_buf[s, h] - delta)).astype(BF16)
            pb = p.astype(BF16)
            grad_q = mm(ds, kc[s, h])
            if i == 0:
                dq_acc[h] = grad_q
            else:
                dq_acc[h] += grad_q
            grad_k = mm(q_t[h], ds) * SCALE
            grad_v = mm(do_t[h], pb)
            parts += [grad_k[:NOPE], grad_v]
            rope = grad_k[NOPE:]
            grad_rope = rope if grad_rope is None else grad_rope + rope
        dkv = jnp.concatenate(parts, axis=0).astype(BF16)
        if meanwhile is not None:
            meanwhile()
        grad = jnp.concatenate([mm(w[...], dkv), grad_rope], axis=0)
        sbuf[s + co] = grad.astype(BF16).reshape(2, 2, 144, 512)
        part = lax.dot_general(
            kbuf[s, :LATENT, :], dkv, (((1,), (1,)), ((), ())), preferred_element_type=F32
        ).reshape(16, 2, 16, 512)
        if i == 0:
            gw[...] = part
        else:
            gw[...] += part
        send()

    def core_send(i):
        a = jnp.where(co == 0, (0, 1, 3, 2)[i], (4, 1, 3, 2)[i])
        return copy(sbuf.at[a, 1 - co], crecv.at[a], s_core.at[i], r_core.at[a], sibling)

    def z_send(c):
        return copy(sbuf.at[0, c], zrecv, s_z.at[c], r_z.at[0], dev((z + 7) % 8, xl, c, xh, y))

    def y_send(a, t):
        to = (y + t) % 4
        return copy(ysum.at[a, :, :, lanes(to)], yrecv.at[a, t - 1], s_y.at[a, t - 1], r_y.at[a, t - 1], dev(z, xl, co, xh, to))

    def finish(a):
        def wait():
            copy(sbuf.at[a, 0], crecv.at[a], s_core.at[0], r_core.at[a], sibling).wait_recv()

        total = sbuf[a, co].astype(F32)
        if a == 4:
            pl.when(co == 0)(wait)
            pl.when(above)(lambda: z_send(0).wait_recv())
            total = total + zrecv[...].astype(F32)
        else:
            wait()
        ysum[a] = (total + crecv[a].astype(F32)).astype(BF16)
        for t in (2, 1, 3):
            y_send(a, t).start()

    def o_send(a, d):
        owner = (2 * chip + 29 + a) % 32
        to = (xh + d) % 2
        k = FIRST_PART[a] + d
        return copy(tbuf.at[a, to], orecv.at[k, co], s_o.at[a, d], r_o.at[k, co], (owner, to * 4 + y))

    def o_each(a, remote, here):
        def both():
            remote(0)
            remote(1)

        if a < 3:
            pl.when(chip > 0)(both)
        else:
            pl.when(co != a - 3)(lambda: remote(0))
            if here is not None:
                pl.when(co == a - 3)(here)
            remote(1)

    def stage(a):
        for t in (1, 2, 3):
            y_send(a, t).wait_recv()
        total = ysum[a, :, :, lanes(y)].astype(F32)
        for t in range(3):
            total = total + yrecv[a, t].astype(F32)
        tbuf[a] = total.astype(BF16)

        def here():
            orecv[FIRST_PART[a], co] = tbuf[a, xh]

        o_each(a, lambda d: o_send(a, d).start(), here)

    def g1():
        return copy(gw.at[:, 1 - co], g1recv, s_g.at[0], r_g.at[0], sibling)

    def g2():
        return copy(g2buf.at[:, 1 - xl], g2recv, s_g.at[1], r_g.at[1], dev(z, 1 - xl, co, xh, y))

    def g3(t):
        to = (z + t) % 8
        return copy(g3buf.at[to], g3recv.at[t - 1], s_g.at[1 + t], r_g.at[1 + t], dev(to, xl, co, xh, y))

    def arrived(k, c):
        copy(tbuf.at[0, 0], orecv.at[k, c], s_o.at[0, 0], r_o.at[k, c], sibling).wait_recv()

    def ag(t):
        return copy(
            fin, out_ref.at[:, xh, :, lanes(y)], s_ag.at[t - 1], r_ag.at[t - 1], (ctx, (head + t) % 8)
        )

    def mine_out():
        return pltpu.make_async_copy(fin, out_ref.at[:, xh, :, lanes(y)], s_out.at[2])

    def final(count, parts):
        @pl.when(chip < 15)
        def _():
            for k, c in parts[0]:
                arrived(k, c)

        for k, c in parts[1]:
            arrived(k, c)
        total = orecv[0].astype(F32)
        for k in range(1, count):
            total = total + orecv[k].astype(F32)
        fin[...] = total.astype(BF16)
        for t in (2, 6, 1, 7, 3, 5, 4):
            ag(t).start()
        mine_out().start()

    def send_first():
        @pl.when((co == 0) & below)
        def _():
            z_send(0).start()
            z_send(1).start()

        @pl.when(co == 1)
        def _():
            core_send(0).start()

    second(0, send_first)
    hear(1)
    tell(2)
    second(1, lambda: core_send(1).start())
    second(2, lambda: core_send(2).start(), lambda: finish(1))
    second(3, lambda: core_send(3).start(), lambda: finish(3))
    g1().start()
    finish(2)
    g1().wait_recv()
    g2buf[...] = (gw[:, co] + g1recv[...]).astype(BF16).reshape(8, 2, 16, 512)
    g2().start()
    stage(1)
    finish(4)
    stage(3)

    stage(2)
    stage(4)

    @pl.when(co == 0)
    def _():
        final(4, ([(0, 0), (0, 1), (1, 0), (1, 1)], [(2, 1), (3, 0), (3, 1)]))

    @pl.when(co == 1)
    def _():
        final(4, ([(0, 0), (0, 1), (1, 0), (1, 1)], [(2, 0), (3, 0), (3, 1)]))

    g2().wait_recv()
    g3buf[...] = (g2buf[:, xl].astype(F32) + g2recv[...].astype(F32)).astype(BF16)
    hear(2)
    for t in range(1, 8):
        g3(t).start()
    for h in range(HEADS):
        dq_ref[:, h * 192 : (h + 1) * 192] = (dq_acc[h] * SCALE).astype(BF16)
    dq_out = pltpu.make_async_copy(dq_ref, dq_hbm, s_out.at[0])
    dq_out.start()
    for t in range(1, 8):
        g3(t).wait_recv()
    total = g3buf[z].astype(F32)
    for t in range(7):
        total = total + g3recv[t].astype(F32)
    gwo_ref[...] = total
    gw_out = pltpu.make_async_copy(gwo_ref, gwo_hbm, s_out.at[1])
    gw_out.start()
    for t in range(1, 8):
        ag(t).wait_recv()

    mine_out().wait()
    dq_out.wait()
    gw_out.wait()
    pl.when(sends_full)(lambda: full().wait_send())
    pl.when((xl == 1) & (co == 0) & above)(lambda: piece().wait_send())

    @pl.when((xl == 1) & below)
    def _():
        for t in range(8):
            relay(t).wait_send()

    @pl.when(xl == 1)
    def _():
        for d in range(2):
            pass_half(d).wait_send()

    @pl.when(xl == 0)
    def _():
        half(0).wait_send()
        half(1).wait_send()

    @pl.when((xl == 0) & below)
    def _():
        for t in range(8):
            pass_piece(t).wait_send()

    @pl.when((co == 0) & below)
    def _():
        z_send(0).wait_send()
        z_send(1).wait_send()

    @pl.when(co == 1)
    def _():
        core_send(0).wait_send()

    for i in range(1, 4):
        core_send(i).wait_send()
    for a in range(1, 5):
        for t in (1, 2, 3):
            y_send(a, t).wait_send()
        o_each(a, lambda d: o_send(a, d).wait_send(), None)
    g1().wait_send()
    g2().wait_send()
    for t in range(1, 8):
        g3(t).wait_send()
        ag(t).wait_send()


def place(dq, out, gwo, dq_ref, out_ref, gwo_ref, dq_v, out_v, gwo_v, sem):
    held = ((dq, dq_v, dq_ref), (out, out_v, out_ref), (gwo, gwo_v, gwo_ref))
    come = [pltpu.make_async_copy(a, b, sem.at[0, i]) for i, (a, b, _) in enumerate(held)]
    go = [pltpu.make_async_copy(b, c, sem.at[1, i]) for i, (_, b, c) in enumerate(held)]
    for c in come:
        c.start()
    for i in range(3):
        come[i].wait()
        go[i].start()
    for c in go:
        c.wait()


def local(kv_latent, queries, grad_out, kv_up_weight, doc_ids):
    vm = pl.BlockSpec(memory_space=pltpu.VMEM)
    hbm = pl.BlockSpec(memory_space=pl.ANY)
    dma = pltpu.SemaphoreType.DMA
    V = pltpu.VMEM
    dq, out, gwo = pl.pallas_call(
        body,
        out_shape=(
            jax.ShapeDtypeStruct((ROWS, HEADS * (NOPE + ROPE)), BF16),
            jax.ShapeDtypeStruct((2, 2, 144, ROWS), BF16),
            jax.ShapeDtypeStruct((16, 512), F32),
        ),
        in_specs=[hbm] * 5,
        out_specs=(hbm, hbm, hbm),
        scratch_shapes=[
            V((ROWS, 384), BF16), V((16, 512), F32), dma((3,)),
            V((4, KEY_ROWS, ROWS), BF16), V((304, 128), BF16), V((2, 144, ROWS), BF16),
            V((ROWS, 384), BF16), V((ROWS, 256), BF16), V((512, 512), BF16), V((8, 128), jnp.int32),
            V((2, ROWS, NOPE + ROPE + MARKS), BF16), V((2, 192, ROWS), BF16), V((2, 128, ROWS), BF16), V((512, 512), BF16),
            V((4, 2, ROWS, 192), BF16), V((4, 2, ROWS, ROWS), F32), V((4, 2, ROWS, ROWS), F32),
            V((2, ROWS, 1), F32), V((2, ROWS, 1), F32), V((2, ROWS, 1), F32), V((4, 2, ROWS, 1), F32),
            V((2, ROWS, 192), F32), V((16, 2, 16, 512), F32),
            V((5, 2, 2, 144, 512), BF16), V((5, 2, 144, 512), BF16), V((5, 2, 144, 512), BF16),
            V((5, 3, 2, 144, 128), BF16),
            V((5, 2, 144, 128), BF16), V((4, 2, 144, 128), BF16), V((2, 144, 128), BF16),
            V((16, 16, 512), F32), V((8, 2, 16, 512), BF16), V((8, 16, 512), BF16), V((8, 16, 512), BF16),
            V((7, 16, 512), BF16),
            dma((5,)), dma((4,)), dma((8,)), dma((8,)), dma((2,)), dma((4,)), dma((5, 3)), dma((5, 2)), dma((7,)),
            dma((9,)),
            dma((3,)), dma((1,)), pltpu.SemaphoreType.REGULAR((3,)), dma((8,)), dma((2,)), dma((1,)),
            dma((5,)), dma((5, 3)), dma((5, 2)), dma((7,)), dma((9,)),
        ],
        compiler_params=pltpu.CompilerParams(
            collective_id=0, has_side_effects=True, vmem_limit_bytes=58 * 1024 * 1024
        ),
        cost_estimate=pl.CostEstimate(flops=7_000_000_000, bytes_accessed=4_000_000, transcendentals=2_100_000),
    )(kv_latent.T, queries, grad_out, kv_up_weight, doc_ids.reshape(128, 128))
    dq, out, gwo = pl.pallas_call(
        place,
        out_shape=(
            jax.ShapeDtypeStruct((ROWS, HEADS * (NOPE + ROPE)), BF16),
            jax.ShapeDtypeStruct((WIDE, ROWS), BF16),
            jax.ShapeDtypeStruct((16, 512), F32),
        ),
        in_specs=[hbm] * 3,
        out_specs=(hbm, hbm, hbm),
        scratch_shapes=[V((ROWS, 384), BF16), V((WIDE, ROWS), BF16), V((16, 512), F32), dma((2, 3))],
    )(dq, out.reshape(WIDE, ROWS), gwo)
    return dq, out.T, gwo


def solution(mesh):
    return jax.shard_map(
        local,
        mesh=mesh,
        in_specs=(P("ctx", None), P("ctx", "head"), P("ctx", "head"), P(None, "head"), P()),
        out_specs=(P("ctx", "head"), P("ctx", None), P("ctx", "head")),
        check_vma=False,
    )
```
